512 devices in a mesh: seq: 32 (over y, x, core), ch: 16 (over z).
Axes of the slice: x: 4, y: 4, z: 16, core: 2. Of those that a mesh axis runs over, the one named last changes fastest.
Arguments:
- q_branch: bfloat16 [16384, 4096], P('seq', 'ch'), may hold values from -6 to 6
- k_branch: bfloat16 [16384, 4096], P('seq', 'ch'), may hold values from -6 to 6
- v_branch: bfloat16 [16384, 4096], P('seq', 'ch'), may hold values from -6 to 6
- decay_rates: float32 [16, 4096], P(None, 'ch'), may hold values from 1.2207031e-05 to 0.05
- residues: float32 [16, 4096], P(None, 'ch'), may hold values from -0.237170825 to 0.237170825
- skip_gain: float32 [4096], P('ch'), may hold values from 0.5 to 1.5
- out_weight: bfloat16 [4096, 4096], P(None, 'ch'), may hold values from -0.09375 to 0.09375
Outputs:
- mixed: bfloat16 [16384, 4096], P('seq', 'ch')
The draws below stay inside these ranges and needn't reach their ends.
All inputs are finite; a program needn't handle non-finite values.
Results may differ from the reference program's by a relative error of at most 0.015.
Values may be sent and summed in bfloat16 or wider, within the bound.
No kernel may reach another device: no remote copies, remote signals or barrier semaphores. Data moves between devices by JAX's collectives and lax.ppermute only.
A program may use at most 64 MiB of HBM per device.

```python
import math
import jax
import jax.numpy as jnp
from jax import lax

D = 4096
MODES = 16
SEQ = 16384


def modal_rates(key, slow_share):
    first_key, second_key, third_key = jax.random.split(key, 3)
    is_slow = jax.random.uniform(first_key, (MODES, D)) < slow_share
    slow_rate = jnp.exp(jax.random.uniform(second_key, (MODES, D), minval=math.log(0.2 / SEQ), maxval=math.log(2.0 / SEQ)))
    fast_rate = jnp.exp(jax.random.uniform(third_key, (MODES, D), minval=math.log(0.02), maxval=math.log(0.05)))
    return jnp.where(is_slow, slow_rate, fast_rate).astype(jnp.float32)


def draw_decay_rates(key, part):
    slow_share = 0.5
    return modal_rates(key, slow_share)


def draw_residues(key, part):
    slow_share = 0.5
    rate_values = modal_rates(key, slow_share)
    key = jax.random.fold_in(key, 11)
    normal_values = jax.random.truncated_normal(key, -3.0, 3.0, (MODES, D), jnp.float32)
    return normal_values * jnp.sqrt(2.0 * rate_values / MODES)


def shard_levels(own_key, extent, cuts, low, high):
    def one(axis_at, parts):
        steps = jax.random.uniform(jax.random.fold_in(jax.random.fold_in(own_key, 6), axis_at), (parts,), jnp.float32, low / len(cuts), high / len(cuts))
        return jnp.repeat(jnp.exp(steps), extent[axis_at] // parts).reshape((-1,) + (1,) * (len(extent) - axis_at - 1))

    loudness = one(*cuts[0])
    for cut in cuts[1:]:
        loudness = loudness * one(*cut)
    return loudness


def gaussian(key, shape, width, limit, shards=(), kind=jnp.bfloat16):
    drawn = jax.random.normal(key, shape, jnp.float32) * width
    if len(shards) > 0:
        drawn = shard_levels(key, shape, shards, -0.22, 0.18) * drawn
    return jnp.clip(drawn, min=-limit, max=limit).astype(kind)


def setup_inputs(seed: int = 0) -> dict:
    splits = jax.random.split(jax.random.key(seed), 8)
    q_branch = gaussian(splits[0], (SEQ, D), 1.0, 6.0, ((0, 32), (1, 16)))
    k_branch = gaussian(splits[1], (SEQ, D), 1.0, 6.0, ((0, 32), (1, 16)))
    v_branch = gaussian(splits[2], (SEQ, D), 1.0, 6.0, ((0, 32), (1, 16)))
    decay_rates = draw_decay_rates(jax.random.fold_in(splits[7], 71), 0)
    residues = draw_residues(jax.random.fold_in(splits[7], 71), 0)
    skip_gain = jnp.clip(0.5 + 1.0 * jax.random.uniform(splits[5], (D,), jnp.float32) ** shard_levels(splits[5], (D,), ((0, 16),), -0.2, 0.2), 0.5, 1.5)
    out_weight = gaussian(splits[6], (D, D), D ** -0.5, 0.09375, ((1, 16),))
    return {"q_branch": q_branch, "k_branch": k_branch, "v_branch": v_branch, "decay_rates": decay_rates, "residues": residues, "skip_gain": skip_gain, "out_weight": out_weight}


def reference(q_branch, k_branch, v_branch, decay_rates, residues, skip_gain, out_weight):
    mixed_in = (k_branch.astype(jnp.float32) * v_branch.astype(jnp.float32)).astype(jnp.bfloat16)
    width_block = min(256, D)
    groups = D // width_block
    positions = jnp.arange(SEQ, dtype=jnp.float32)

    def convolve(operands):
        signal, rate_block, resid_block = operands
        kernel = jnp.zeros((SEQ, width_block), jnp.float32)
        for mode_idx in range(MODES):
            kernel = kernel + resid_block[mode_idx][None, :] * jnp.exp(-rate_block[mode_idx][None, :] * positions[:, None])
        product = jnp.fft.rfft(kernel, n=2 * SEQ, axis=0) * jnp.fft.rfft(signal, n=2 * SEQ, axis=0)
        return jnp.fft.irfft(product, n=2 * SEQ, axis=0)[:SEQ].astype(jnp.float32)

    signal_all = mixed_in.astype(jnp.float32).reshape(SEQ, groups, width_block).transpose(1, 0, 2)
    rate_all = decay_rates.reshape(MODES, groups, width_block).transpose(1, 0, 2)
    resid_all = residues.reshape(MODES, groups, width_block).transpose(1, 0, 2)
    conv = lax.map(convolve, (signal_all, rate_all, resid_all))
    conv = conv.transpose(1, 0, 2).reshape(SEQ, D)
    gated = (q_branch.astype(jnp.float32) * (conv + skip_gain[None, :] * mixed_in.astype(jnp.float32))).astype(jnp.bfloat16)
    return jnp.dot(gated, out_weight, preferred_element_type=jnp.float32).astype(jnp.bfloat16)
```

```python
import jax
import jax.numpy as jnp
from jax import lax
from jax.experimental import pallas as pl
from jax.experimental.pallas import tpu as pltpu
from jax.sharding import Mesh
from jax.sharding import PartitionSpec as P

BLOCKS = 8
LANES = 128
F32 = jnp.float32
BF16 = jnp.bfloat16


def fill_natural(core, own_ref, oth_ref, flat):
    rows = own_ref.shape[0]
    piece = 64
    own_at, oth_at = core * rows, (1 - core) * rows

    @pl.loop(0, rows // piece)
    def _(i):
        at = pl.multiple_of(i * piece, piece)
        for half in range(flat.shape[0]):
            lanes = slice(half * LANES, (half + 1) * LANES)
            flat[half, pl.ds(pl.multiple_of(own_at + at, piece), piece), :] = own_ref[pl.ds(at, piece), lanes].astype(F32)
            flat[half, pl.ds(pl.multiple_of(oth_at + at, piece), piece), :] = oth_ref[pl.ds(at, piece), lanes].astype(F32)


def spread(ref, mode, lanes):
    return jnp.broadcast_to(ref[mode : mode + 1, lanes], (BLOCKS, LANES))


def states_kernel(core_ref, own_ref, oth_ref, rates_ref, total_ref, ends_ref, flat):
    modes, width = rates_ref.shape
    steps = flat.shape[1] // BLOCKS
    fill_natural(core_ref[0], own_ref, oth_ref, flat)
    block = lax.broadcasted_iota(jnp.int32, (BLOCKS, LANES), 0).astype(F32)
    for half in range(width // LANES):
        lanes = slice(half * LANES, (half + 1) * LANES)
        poles = [jnp.exp(-spread(rates_ref, m, lanes)) for m in range(modes)]

        def step(j, held):
            now = flat[half, pl.ds(j, BLOCKS, stride=steps), :]
            return tuple(p * h + now for p, h in zip(poles, held))

        held = lax.fori_loop(0, steps, step, (jnp.zeros((BLOCKS, LANES), F32),) * modes, unroll=8)
        for m in range(modes):
            ends_ref[m, :, lanes] = held[m]
            fade = jnp.exp(-spread(rates_ref, m, lanes) * (steps * (BLOCKS - 1 - block)))
            total_ref[m : m + 1, lanes] = jnp.sum(fade * held[m], axis=0, keepdims=True)


def local_kernel(core_ref, own_ref, oth_ref, q_own_ref, q_oth_ref, rates_ref, resid_ref, skip_ref, ends_ref, conv_ref, gate_ref, flat, flat_q):
    modes, width = rates_ref.shape
    steps = flat.shape[1] // BLOCKS
    fill_natural(core_ref[0], own_ref, oth_ref, flat)
    fill_natural(core_ref[0], q_own_ref, q_oth_ref, flat_q)
    block = lax.broadcasted_iota(jnp.int32, (BLOCKS, LANES), 0)
    for half in range(width // LANES):
        lanes = slice(half * LANES, (half + 1) * LANES)
        poles, weights, first = [], [], []
        for m in range(modes):
            rate = spread(rates_ref, m, lanes)
            poles.append(jnp.exp(-rate))
            weights.append(spread(resid_ref, m, lanes))
            scan = ends_ref[m, :, lanes]
            for shift in (1, 2, 4):
                moved = jnp.where(block >= shift, pltpu.roll(scan, shift, 0), 0.0)
                scan = scan + jnp.exp(-rate * float(steps * shift)) * moved
            first.append(jnp.where(block >= 1, pltpu.roll(scan, 1, 0), 0.0))
        direct = jnp.broadcast_to(skip_ref[0:1, lanes], (BLOCKS, LANES))

        def step(j, held):
            now = flat[half, pl.ds(j, BLOCKS, stride=steps), :]
            held = tuple(p * h + now for p, h in zip(poles, held))
            terms = [w * h for w, h in zip(weights, held)]
            while len(terms) > 1:
                terms = [a + b for a, b in zip(terms[::2], terms[1::2])]
            conv_ref[j, :, lanes] = terms[0] + direct * now
            gate_ref[j, :, lanes] = flat_q[half, pl.ds(j, BLOCKS, stride=steps), :]
            return held

        lax.fori_loop(0, steps, step, tuple(first), unroll=4)


def gate_kernel(place_ref, all_ref, rates_ref, resid_ref, conv_ref, gate_ref, own_ref, oth_ref, flat):
    chips, modes, width = all_ref.shape
    steps = conv_ref.shape[0]
    chip, core = place_ref[0], place_ref[1]
    block = lax.broadcasted_iota(jnp.int32, (BLOCKS, LANES), 0).astype(F32)
    rates = rates_ref[...]
    fade = jnp.exp(-rates * float(steps * BLOCKS))
    before = jnp.zeros((modes, width), F32)
    for c in range(chips - 1):
        before = jnp.where(c < chip, fade * before + all_ref[c], before)
    before = before * resid_ref[...]
    for half in range(width // LANES):
        lanes = slice(half * LANES, (half + 1) * LANES)
        poles, first = [], []
        for m in range(modes):
            rate = spread(rates_ref, m, lanes)
            poles.append(jnp.exp(-rate))
            come = jnp.broadcast_to(before[m : m + 1, lanes], (BLOCKS, LANES))
            first.append(come * jnp.exp(-rate * (steps * block + 1.0)))

        def step(j, held):
            terms = list(held)
            while len(terms) > 1:
                terms = [a + b for a, b in zip(terms[::2], terms[1::2])]
            flat[half, pl.ds(j, BLOCKS, stride=steps), :] = gate_ref[j, :, lanes] * (conv_ref[j, :, lanes] + terms[0])
            return tuple(p * h for p, h in zip(poles, held))

        lax.fori_loop(0, steps, step, tuple(first), unroll=4)
    rows = own_ref.shape[0]
    piece = 64
    own_at, oth_at = core * rows, (1 - core) * rows

    @pl.loop(0, rows // piece)
    def _(i):
        at = pl.multiple_of(i * piece, piece)
        for half in range(flat.shape[0]):
            lanes = slice(half * LANES, (half + 1) * LANES)
            own_ref[pl.ds(at, piece), lanes] = flat[half, pl.ds(pl.multiple_of(own_at + at, piece), piece), :].astype(BF16)
            oth_ref[pl.ds(at, piece), lanes] = flat[half, pl.ds(pl.multiple_of(oth_at + at, piece), piece), :].astype(BF16)


VMEM = pl.BlockSpec(memory_space=pltpu.VMEM)
SMEM = pl.BlockSpec(memory_space=pltpu.SMEM)
PARAMS = pltpu.CompilerParams(vmem_limit_bytes=40 * 1024 * 1024)


def body(q_branch, k_branch, v_branch, decay_rates, residues, skip_gain, out_weight):
    rows, width = k_branch.shape
    modes = decay_rates.shape[0]
    steps = 2 * rows // BLOCKS
    chips = lax.axis_size("y") * lax.axis_size("x")
    depth = lax.axis_size("ch")
    core, z = lax.axis_index("core"), lax.axis_index("ch")
    chip = lax.axis_index("y") * lax.axis_size("x") + lax.axis_index("x")
    core_at = core.reshape(1).astype(jnp.int32)
    place = jnp.stack([chip, core]).astype(jnp.int32)
    shape = lambda s, d=F32: jax.ShapeDtypeStruct(s, d)
    swap = [(0, 1), (1, 0)]

    mixed_in = (k_branch.astype(F32) * v_branch.astype(F32)).astype(BF16)
    x_oth, q_oth = lax.ppermute(jnp.stack([mixed_in, q_branch]), "core", swap)

    total, ends = pl.pallas_call(
        states_kernel,
        out_shape=(shape((modes, width)), shape((modes, BLOCKS, width))),
        in_specs=[SMEM, VMEM, VMEM, VMEM],
        out_specs=(VMEM, VMEM),
        scratch_shapes=[pltpu.VMEM((width // LANES, 2 * rows, LANES), F32)],
        compiler_params=PARAMS,
        name="chip_states",
    )(core_at, mixed_in, x_oth, decay_rates)

    every = lax.all_to_all(
        jnp.broadcast_to(total[None], (chips, modes, width)), ("y", "x"), split_axis=0, concat_axis=0, tiled=True
    )
    conv, gate = pl.pallas_call(
        local_kernel,
        out_shape=(shape((steps, BLOCKS, width)), shape((steps, BLOCKS, width))),
        in_specs=[SMEM] + [VMEM] * 8,
        out_specs=(VMEM, VMEM),
        scratch_shapes=[pltpu.VMEM((width // LANES, 2 * rows, LANES), F32)] * 2,
        compiler_params=PARAMS,
        cost_estimate=pl.CostEstimate(flops=4 * modes * 2 * rows * width, bytes_accessed=4 << 20, transcendentals=0),
        name="chip_convolution",
    )(core_at, mixed_in, x_oth, q_branch, q_oth, decay_rates, residues, skip_gain[None, :], ends)

    own, oth = pl.pallas_call(
        gate_kernel,
        out_shape=(shape((rows, width), BF16), shape((rows, width), BF16)),
        in_specs=[SMEM] + [VMEM] * 5,
        out_specs=(VMEM, VMEM),
        scratch_shapes=[pltpu.VMEM((width // LANES, 2 * rows, LANES), F32)],
        compiler_params=PARAMS,
        name="carry_and_gate",
    )(place, every, decay_rates, residues, conv, gate)

    ring = [(c * depth + i, c * depth + (i + 1 - 2 * c) % depth) for c in range(2) for i in range(depth)]
    hop = lambda array: lax.ppermute(array, ("core", "ch"), ring)

    def project(array, distance):
        source = lax.rem(z + (2 * core - 1) * distance + depth, depth)
        weight = lax.dynamic_slice(out_weight, (source * width, 0), (width, out_weight.shape[1]))
        return jnp.dot(array, weight, preferred_element_type=F32)

    sum_own, sum_oth = project(own, 0), None
    for distance in range(1, depth // 2):
        own, oth = hop(own), hop(oth)
        sum_own = sum_own + project(own, distance)
        part = project(oth, distance)
        sum_oth = part if sum_oth is None else sum_oth + part
    own = hop(own)
    sum_own = sum_own + lax.ppermute(sum_oth, "core", swap) + project(own, depth // 2)
    return sum_own.astype(BF16)


def solution(mesh):
    chips = Mesh(mesh.devices.reshape(4, 4, 2, 16), ("y", "x", "core", "ch"))
    seq = ("y", "x", "core")
    placed = (P(seq, "ch"), P(seq, "ch"), P(seq, "ch"), P(None, "ch"), P(None, "ch"), P("ch"), P(None, "ch"))
    return jax.shard_map(body, mesh=chips, in_specs=placed, out_specs=P(seq, "ch"), check_vma=False)
```

```python
import jax
import jax.numpy as jnp
from jax import lax
from jax.experimental import pallas as pl
from jax.experimental.pallas import tpu as pltpu
from jax.sharding import Mesh
from jax.sharding import PartitionSpec as P

BLOCKS = 8
LANES = 128
F32 = jnp.float32
BF16 = jnp.bfloat16


def spread(ref, mode, lanes):
    return jnp.broadcast_to(ref[mode : mode + 1, lanes], (BLOCKS, LANES))


def tree_sum(terms):
    terms = list(terms)
    while len(terms) > 1:
        terms = [a + b for a, b in zip(terms[::2], terms[1::2])]
    return terms[0]


def fetch(pairs, sems):
    copies = [pltpu.make_async_copy(source, target, sems.at[i]) for i, (source, target) in enumerate(pairs)]
    for copy in copies:
        copy.start()
    return copies


def fill(flat, rows, value):
    piece = 64

    @pl.loop(0, rows // piece)
    def _(i):
        at = pl.ds(pl.multiple_of(i * piece, piece), piece)
        now = value(at)
        for half in range(flat.shape[0]):
            flat[half, at, :] = now[:, half * LANES : (half + 1) * LANES]


def mixed_in(k_ref, v_ref):
    return lambda at: (k_ref[at, :].astype(F32) * v_ref[at, :].astype(F32)).astype(BF16).astype(F32)


def block_ends(flat, rates_ref, half):
    modes, steps = rates_ref.shape[0], flat.shape[1] // BLOCKS
    lanes = slice(half * LANES, (half + 1) * LANES)
    poles = [jnp.exp(-spread(rates_ref, m, lanes)) for m in range(modes)]

    def step(j, held):
        now = flat[half, pl.ds(j, BLOCKS, stride=steps), :]
        return tuple(p * h + now for p, h in zip(poles, held))

    return poles, lax.fori_loop(0, steps, step, (jnp.zeros((BLOCKS, LANES), F32),) * modes, unroll=8)


def states_kernel(k_hbm, v_hbm, rates_hbm, total_ref, flat, k_ref, v_ref, rates_ref, sems):
    modes, width = rates_ref.shape
    rows = k_ref.shape[0]
    steps = rows // BLOCKS
    for copy in fetch(((rates_hbm, rates_ref), (k_hbm, k_ref), (v_hbm, v_ref)), sems):
        copy.wait()
    fill(flat, rows, mixed_in(k_ref, v_ref))
    block = lax.broadcasted_iota(jnp.int32, (BLOCKS, LANES), 0).astype(F32)
    for half in range(width // LANES):
        lanes = slice(half * LANES, (half + 1) * LANES)
        _, held = block_ends(flat, rates_ref, half)
        for m in range(modes):
            fade = jnp.exp(-spread(rates_ref, m, lanes) * (steps * (BLOCKS - 1 - block)))
            total_ref[m : m + 1, lanes] = jnp.sum(fade * held[m], axis=0, keepdims=True)


def local_kernel(core_ref, k_hbm, v_hbm, q_hbm, rates_hbm, resid_hbm, skip_hbm, oth_hbm, out_hbm, flat, flat_q, k_ref, v_ref, q_ref, rates_ref, resid_ref, oth_ref, skip_ref, out_ref, sems):
    modes, width = rates_ref.shape
    rows = q_ref.shape[0]
    steps = rows // BLOCKS
    pairs = ((rates_hbm, rates_ref), (resid_hbm, resid_ref), (skip_hbm, skip_ref), (oth_hbm, oth_ref))
    for copy in fetch(pairs + ((k_hbm, k_ref), (v_hbm, v_ref), (q_hbm, q_ref)), sems):
        copy.wait()
    fill(flat, rows, mixed_in(k_ref, v_ref))
    fill(flat_q, rows, lambda at: q_ref[at, :].astype(F32))
    block = lax.broadcasted_iota(jnp.int32, (BLOCKS, LANES), 0)
    second = (core_ref[0] > 0).astype(F32)
    for half in range(width // LANES):
        lanes = slice(half * LANES, (half + 1) * LANES)
        poles, held = block_ends(flat, rates_ref, half)
        weights, first = [], []
        for m in range(modes):
            rate = spread(rates_ref, m, lanes)
            weights.append(spread(resid_ref, m, lanes))
            come = second * spread(oth_ref, m, lanes)
            scan = jnp.where(block >= 1, pltpu.roll(held[m], 1, 0), come)
            for shift in (1, 2, 4):
                moved = jnp.where(block >= shift, pltpu.roll(scan, shift, 0), 0.0)
                scan = scan + jnp.exp(-rate * float(steps * shift)) * moved
            first.append(scan)
        direct = spread(skip_ref, 0, lanes)

        def step(j, held):
            now = flat[half, pl.ds(j, BLOCKS, stride=steps), :]
            held = tuple(p * h + now for p, h in zip(poles, held))
            out_ref[j, 0:BLOCKS, lanes] = tree_sum(w * h for w, h in zip(weights, held)) + direct * now
            out_ref[j, BLOCKS : 2 * BLOCKS, lanes] = flat_q[half, pl.ds(j, BLOCKS, stride=steps), :]
            return held

        lax.fori_loop(0, steps, step, tuple(first), unroll=4)
    copy = pltpu.make_async_copy(out_ref, out_hbm, sems.at[7])
    copy.start()
    copy.wait()


def gate_kernel(core_ref, chip_ref, all_hbm, rates_hbm, resid_hbm, local_hbm, out_hbm, flat, all_ref, rates_ref, resid_ref, local_ref, out_ref, sems):
    chips, modes, width = all_ref.shape
    steps = local_ref.shape[0]
    rows = out_ref.shape[0]
    small = fetch(((rates_hbm, rates_ref), (resid_hbm, resid_ref), (all_hbm, all_ref), (local_hbm, local_ref)), sems)
    large = small.pop()
    for copy in small:
        copy.wait()
    chip, core = chip_ref[0], core_ref[0]
    block = lax.broadcasted_iota(jnp.int32, (BLOCKS, LANES), 0).astype(F32)
    rates = rates_ref[...]
    fade = jnp.exp(-rates * float(2 * rows))
    before = jnp.zeros((modes, width), F32)
    for c in range(chips - 1):
        before = jnp.where(c < chip, fade * before + all_ref[c], before)
    before = jnp.where(core == 0, before, jnp.exp(-rates * float(rows)) * before)
    before = before * resid_ref[...]
    sent = []
    for half in range(width // LANES):
        lanes = slice(half * LANES, (half + 1) * LANES)
        poles, first = [], []
        for m in range(modes):
            rate = spread(rates_ref, m, lanes)
            poles.append(jnp.exp(-rate))
            come = jnp.broadcast_to(before[m : m + 1, lanes], (BLOCKS, LANES))
            first.append(come * jnp.exp(-rate * (steps * block + 1.0)))
        if half == 0:
            large.wait()

        def step(j, held):
            conv = local_ref[j, 0:BLOCKS, lanes] + tree_sum(held)
            flat[half, pl.ds(j, BLOCKS, stride=steps), :] = local_ref[j, BLOCKS : 2 * BLOCKS, lanes] * conv
            return tuple(p * h for p, h in zip(poles, held))

        lax.fori_loop(0, steps, step, tuple(first), unroll=4)
        piece = 64

        @pl.loop(0, rows // piece)
        def _(i):
            at = pl.ds(pl.multiple_of(i * piece, piece), piece)
            out_ref[at, lanes] = flat[half, at, :].astype(BF16)

        sent.append(pltpu.make_async_copy(out_ref.at[:, lanes], out_hbm.at[:, lanes], sems.at[4 + half]))
        sent[-1].start()
    for copy in sent:
        copy.wait()


VMEM = pl.BlockSpec(memory_space=pltpu.VMEM)
ANY = pl.BlockSpec(memory_space=pl.ANY)
SMEM = pl.BlockSpec(memory_space=pltpu.SMEM)


def kernel_call(kernel, name, cost, **kwargs):
    return pl.pallas_call(
        kernel,
        name=name,
        cost_estimate=pl.CostEstimate(flops=cost, bytes_accessed=1 << 20, transcendentals=0),
        **kwargs,
    )


def body(q_branch, k_branch, v_branch, decay_rates, residues, skip_gain, out_weight):
    rows, width = k_branch.shape
    modes = decay_rates.shape[0]
    steps = rows // BLOCKS
    chips = lax.axis_size("y") * lax.axis_size("x")
    depth = lax.axis_size("ch")
    core, z = lax.axis_index("core"), lax.axis_index("ch")
    chip = lax.axis_index("y") * lax.axis_size("x") + lax.axis_index("x")
    core_at = core.reshape(1).astype(jnp.int32)
    chip_at = chip.reshape(1).astype(jnp.int32)
    shape = lambda s, d=F32: jax.ShapeDtypeStruct(s, d)
    flat_shape = (width // LANES, rows, LANES)
    work = modes * rows * width
    swap = lambda array: lax.ppermute(array, "core", [(0, 1), (1, 0)])

    flat_of = pltpu.VMEM(flat_shape, F32)
    half_of = pltpu.VMEM((rows, width), BF16)
    modal = pltpu.VMEM((modes, width), F32)
    sems = lambda count: pltpu.SemaphoreType.DMA((count,))

    by_step = (steps, 2 * BLOCKS, width)
    total = kernel_call(
        states_kernel,
        "states",
        2 * work,
        out_shape=shape((modes, width)),
        in_specs=[ANY] * 3,
        out_specs=VMEM,
        scratch_shapes=[flat_of, half_of, half_of, modal, sems(3)],
    )(k_branch, v_branch, decay_rates)
    total_oth = swap(total)
    first = core == 0
    every = jnp.exp(-decay_rates * float(rows)) * jnp.where(first, total, total_oth) + jnp.where(first, total_oth, total)
    every = jnp.broadcast_to(every[None], (chips, modes, width))
    every = lax.all_to_all(every, ("y", "x"), split_axis=0, concat_axis=0, tiled=True)
    local = kernel_call(
        local_kernel,
        "chip_convolution",
        6 * work,
        out_shape=shape(by_step),
        in_specs=[SMEM] + [ANY] * 6 + [ANY],
        out_specs=ANY,
        scratch_shapes=[flat_of, flat_of, half_of, half_of, half_of, modal, modal, modal]
        + [pltpu.VMEM((1, width), F32), pltpu.VMEM(by_step, F32), sems(8)],
    )(core_at, k_branch, v_branch, q_branch, decay_rates, residues, skip_gain[None, :], total_oth)
    own = kernel_call(
        gate_kernel,
        "carry_and_gate",
        2 * work,
        out_shape=shape((rows, width), BF16),
        in_specs=[SMEM, SMEM] + [ANY] * 4,
        out_specs=ANY,
        scratch_shapes=[flat_of, pltpu.VMEM((chips, modes, width), F32), modal, modal]
        + [pltpu.VMEM(by_step, F32), half_of, sems(4 + width // LANES)],
    )(core_at, chip_at, every, decay_rates, residues, local)

    ring = [(c * depth + i, c * depth + (i + 1 - 2 * c) % depth) for c in range(2) for i in range(depth)]
    cross = [((1 - c) * depth + i, c * depth + (i + 1 - 2 * c) % depth) for c in range(2) for i in range(depth)]
    hop = lambda array, pairs=ring: lax.ppermute(array, ("core", "ch"), pairs)

    def project(array, distance):
        source = lax.rem(z + (2 * core - 1) * distance + depth, depth)
        weight = lax.dynamic_slice(out_weight, (source * width, 0), (width, out_weight.shape[1]))
        return jnp.dot(array, weight, preferred_element_type=F32)

    sum_own = project(own, 0)
    own, oth = hop(own), hop(own, cross)
    sum_own, sum_oth = sum_own + project(own, 1), project(oth, 1)
    last_oth = oth
    for distance in range(2, depth // 2):
        last_own = own
        own = hop(own)
        oth, last_own = lax.optimization_barrier((oth, last_own))
        last_oth, oth = oth, hop(oth)
        own, last_oth = lax.optimization_barrier((own, last_oth))
        sum_own = sum_own + project(own, distance)
        sum_oth = sum_oth + project(oth, distance)
    last_own, own = own, hop(own, ring[depth:])
    oth, last_own = lax.optimization_barrier((oth, last_own))
    oth = hop(oth, ring[depth:])
    sum_own = sum_own + project(own, depth // 2)
    sum_oth = sum_oth + project(oth, depth // 2)
    sum_oth, sum_own = lax.optimization_barrier((sum_oth, sum_own))
    return (sum_own + swap(sum_oth)).astype(BF16)


def solution(mesh):
    chips = Mesh(mesh.devices.reshape(4, 4, 2, 16), ("y", "x", "core", "ch"))
    seq = ("y", "x", "core")
    placed = (P(seq, "ch"), P(seq, "ch"), P(seq, "ch"), P(None, "ch"), P(None, "ch"), P("ch"), P(None, "ch"))
    return jax.shard_map(body, mesh=chips, in_specs=placed, out_specs=P(seq, "ch"), check_vma=False)
```

```python
import jax
import jax.numpy as jnp
from jax import lax
from jax.experimental import pallas as pl
from jax.experimental.pallas import tpu as pltpu
from jax.sharding import Mesh
from jax.sharding import PartitionSpec as P

BLOCKS = 8
LANES = 128
F32 = jnp.float32
BF16 = jnp.bfloat16


def spread(ref, mode, lanes):
    return jnp.broadcast_to(ref[mode : mode + 1, lanes], (BLOCKS, LANES))


def tree_sum(terms):
    terms = list(terms)
    while len(terms) > 1:
        terms = [a + b for a, b in zip(terms[::2], terms[1::2])]
    return terms[0]


def fetch(pairs, sems):
    copies = [pltpu.make_async_copy(source, target, sems.at[i]) for i, (source, target) in enumerate(pairs)]
    for copy in copies:
        copy.start()
    return copies


def fill(flat, rows, value):
    piece = 64

    @pl.loop(0, rows // piece)
    def _(i):
        at = pl.ds(pl.multiple_of(i * piece, piece), piece)
        now = value(at)
        for half in range(flat.shape[0]):
            flat[half, at, :] = now[:, half * LANES : (half + 1) * LANES]


def mixed_in(k_ref, v_ref):
    return lambda at: (k_ref[at, :].astype(F32) * v_ref[at, :].astype(F32)).astype(BF16).astype(F32)


def block_ends(flat, rates_ref, half):
    modes, steps = rates_ref.shape[0], flat.shape[1] // BLOCKS
    lanes = slice(half * LANES, (half + 1) * LANES)
    poles = [jnp.exp(-spread(rates_ref, m, lanes)) for m in range(modes)]

    def step(j, held):
        now = flat[half, pl.ds(j, BLOCKS, stride=steps), :]
        return tuple(p * h + now for p, h in zip(poles, held))

    return poles, lax.fori_loop(0, steps, step, (jnp.zeros((BLOCKS, LANES), F32),) * modes, unroll=8)


def states_kernel(k_hbm, v_hbm, rates_hbm, total_ref, flat, k_ref, v_ref, rates_ref, sems):
    modes, width = rates_ref.shape
    rows = k_ref.shape[0]
    steps = rows // BLOCKS
    for copy in fetch(((rates_hbm, rates_ref), (k_hbm, k_ref), (v_hbm, v_ref)), sems):
        copy.wait()
    fill(flat, rows, mixed_in(k_ref, v_ref))
    block = lax.broadcasted_iota(jnp.int32, (BLOCKS, LANES), 0).astype(F32)
    for half in range(width // LANES):
        lanes = slice(half * LANES, (half + 1) * LANES)
        _, held = block_ends(flat, rates_ref, half)
        for m in range(modes):
            fade = jnp.exp(-spread(rates_ref, m, lanes) * (steps * (BLOCKS - 1 - block)))
            total_ref[m : m + 1, lanes] = jnp.sum(fade * held[m], axis=0, keepdims=True)


def local_kernel(core_ref, k_hbm, v_hbm, q_hbm, rates_hbm, resid_hbm, skip_hbm, oth_hbm, out_hbm, flat, flat_q, k_ref, v_ref, q_ref, rates_ref, resid_ref, oth_ref, skip_ref, out_ref, sems):
    modes, width = rates_ref.shape
    rows = q_ref.shape[0]
    steps = rows // BLOCKS
    pairs = ((rates_hbm, rates_ref), (resid_hbm, resid_ref), (skip_hbm, skip_ref), (oth_hbm, oth_ref))
    for copy in fetch(pairs + ((k_hbm, k_ref), (v_hbm, v_ref), (q_hbm, q_ref)), sems):
        copy.wait()
    fill(flat, rows, mixed_in(k_ref, v_ref))
    fill(flat_q, rows, lambda at: q_ref[at, :].astype(F32))
    block = lax.broadcasted_iota(jnp.int32, (BLOCKS, LANES), 0)
    second = (core_ref[0] > 0).astype(F32)
    for half in range(width // LANES):
        lanes = slice(half * LANES, (half + 1) * LANES)
        poles, held = block_ends(flat, rates_ref, half)
        weights, first = [], []
        for m in range(modes):
            rate = spread(rates_ref, m, lanes)
            weights.append(spread(resid_ref, m, lanes))
            come = second * spread(oth_ref, m, lanes)
            scan = jnp.where(block >= 1, pltpu.roll(held[m], 1, 0), come)
            for shift in (1, 2, 4):
                moved = jnp.where(block >= shift, pltpu.roll(scan, shift, 0), 0.0)
                scan = scan + jnp.exp(-rate * float(steps * shift)) * moved
            first.append(scan)
        direct = spread(skip_ref, 0, lanes)

        def step(j, held):
            now = flat[half, pl.ds(j, BLOCKS, stride=steps), :]
            held = tuple(p * h + now for p, h in zip(poles, held))
            out_ref[j, 0:BLOCKS, lanes] = tree_sum(w * h for w, h in zip(weights, held)) + direct * now
            out_ref[j, BLOCKS : 2 * BLOCKS, lanes] = flat_q[half, pl.ds(j, BLOCKS, stride=steps), :]
            return held

        lax.fori_loop(0, steps, step, tuple(first), unroll=4)
    copy = pltpu.make_async_copy(out_ref, out_hbm, sems.at[7])
    copy.start()
    copy.wait()


def gate_kernel(core_ref, chip_ref, all_hbm, rates_hbm, resid_hbm, local_hbm, out_hbm, flat, all_ref, rates_ref, resid_ref, local_ref, out_ref, sems):
    chips, modes, width = all_ref.shape
    steps = local_ref.shape[0]
    rows = out_ref.shape[0]
    small = fetch(((rates_hbm, rates_ref), (resid_hbm, resid_ref), (all_hbm, all_ref), (local_hbm, local_ref)), sems)
    large = small.pop()
    for copy in small:
        copy.wait()
    chip, core = chip_ref[0], core_ref[0]
    block = lax.broadcasted_iota(jnp.int32, (BLOCKS, LANES), 0).astype(F32)
    rates = rates_ref[...]
    fade = jnp.exp(-rates * float(2 * rows))
    before = jnp.zeros((modes, width), F32)
    for c in range(chips - 1):
        before = jnp.where(c < chip, fade * before + all_ref[c], before)
    before = jnp.where(core == 0, before, jnp.exp(-rates * float(rows)) * before)
    before = before * resid_ref[...]
    sent = []
    for half in range(width // LANES):
        lanes = slice(half * LANES, (half + 1) * LANES)
        poles, first = [], []
        for m in range(modes):
            rate = spread(rates_ref, m, lanes)
            poles.append(jnp.exp(-rate))
            come = jnp.broadcast_to(before[m : m + 1, lanes], (BLOCKS, LANES))
            first.append(come * jnp.exp(-rate * (steps * block + 1.0)))
        if half == 0:
            large.wait()

        def step(j, held):
            conv = local_ref[j, 0:BLOCKS, lanes] + tree_sum(held)
            flat[half, pl.ds(j, BLOCKS, stride=steps), :] = local_ref[j, BLOCKS : 2 * BLOCKS, lanes] * conv
            return tuple(p * h for p, h in zip(poles, held))

        lax.fori_loop(0, steps, step, tuple(first), unroll=4)
        piece = 64

        @pl.loop(0, rows // piece)
        def _(i):
            at = pl.ds(pl.multiple_of(i * piece, piece), piece)
            out_ref[at, lanes] = flat[half, at, :].astype(BF16)

        sent.append(pltpu.make_async_copy(out_ref.at[:, lanes], out_hbm.at[:, lanes], sems.at[4 + half]))
        sent[-1].start()
    for copy in sent:
        copy.wait()


VMEM = pl.BlockSpec(memory_space=pltpu.VMEM)
ANY = pl.BlockSpec(memory_space=pl.ANY)
SMEM = pl.BlockSpec(memory_space=pltpu.SMEM)


def kernel_call(kernel, name, cost, **kwargs):
    return pl.pallas_call(
        kernel,
        name=name,
        cost_estimate=pl.CostEstimate(flops=cost, bytes_accessed=1 << 20, transcendentals=0),
        **kwargs,
    )


def body(q_branch, k_branch, v_branch, decay_rates, residues, skip_gain, out_weight):
    rows, width = k_branch.shape
    modes = decay_rates.shape[0]
    steps = rows // BLOCKS
    chips = lax.axis_size("y") * lax.axis_size("x")
    depth = lax.axis_size("ch")
    core, z = lax.axis_index("core"), lax.axis_index("ch")
    chip = lax.axis_index("y") * lax.axis_size("x") + lax.axis_index("x")
    core_at = core.reshape(1).astype(jnp.int32)
    chip_at = chip.reshape(1).astype(jnp.int32)
    shape = lambda s, d=F32: jax.ShapeDtypeStruct(s, d)
    flat_shape = (width // LANES, rows, LANES)
    work = modes * rows * width
    swap = lambda array: lax.ppermute(array, "core", [(0, 1), (1, 0)])

    flat_of = pltpu.VMEM(flat_shape, F32)
    half_of = pltpu.VMEM((rows, width), BF16)
    modal = pltpu.VMEM((modes, width), F32)
    sems = lambda count: pltpu.SemaphoreType.DMA((count,))

    by_step = (steps, 2 * BLOCKS, width)
    total = kernel_call(
        states_kernel,
        "states",
        2 * work,
        out_shape=shape((modes, width)),
        in_specs=[ANY] * 3,
        out_specs=VMEM,
        scratch_shapes=[flat_of, half_of, half_of, modal, sems(3)],
    )(k_branch, v_branch, decay_rates)
    total_oth = swap(total)
    first = core == 0
    every = jnp.exp(-decay_rates * float(rows)) * jnp.where(first, total, total_oth) + jnp.where(first, total_oth, total)
    every = jnp.broadcast_to(every[None], (chips, modes, width))
    every = lax.all_to_all(every, ("y", "x"), split_axis=0, concat_axis=0, tiled=True)
    local = kernel_call(
        local_kernel,
        "chip_convolution",
        6 * work,
        out_shape=shape(by_step),
        in_specs=[SMEM] + [ANY] * 6 + [ANY],
        out_specs=ANY,
        scratch_shapes=[flat_of, flat_of, half_of, half_of, half_of, modal, modal, modal]
        + [pltpu.VMEM((1, width), F32), pltpu.VMEM(by_step, F32), sems(8)],
    )(core_at, k_branch, v_branch, q_branch, decay_rates, residues, skip_gain[None, :], total_oth)
    own = kernel_call(
        gate_kernel,
        "carry_and_gate",
        2 * work,
        out_shape=shape((rows, width), BF16),
        in_specs=[SMEM, SMEM] + [ANY] * 4,
        out_specs=ANY,
        scratch_shapes=[flat_of, pltpu.VMEM((chips, modes, width), F32), modal, modal]
        + [pltpu.VMEM(by_step, F32), half_of, sems(4 + width // LANES)],
    )(core_at, chip_at, every, decay_rates, residues, local)

    ring = [(c * depth + i, c * depth + (i + 1 - 2 * c) % depth) for c in range(2) for i in range(depth)]
    cross = [((1 - c) * depth + i, c * depth + (i + 1 - 2 * c) % depth) for c in range(2) for i in range(depth)]
    across = [(c * depth + i, (1 - c) * depth + (i + 1 - 2 * c) % depth) for c in range(2) for i in range(depth)]
    hop = lambda array, pairs=ring: lax.ppermute(array, ("core", "ch"), pairs)

    def project(array, distance):
        source = lax.rem(z + (2 * core - 1) * distance + depth, depth)
        weight = lax.dynamic_slice(out_weight, (source * width, 0), (width, out_weight.shape[1]))
        return jnp.dot(array, weight, preferred_element_type=F32)

    sum_own = project(own, 0)
    own, oth = hop(own), hop(own, cross)
    sum_own, sum_oth = sum_own + project(own, 1), project(oth, 1)
    last_oth = oth
    for distance in range(2, depth // 2 - 1):
        last_own = own
        own = hop(own)
        oth, last_own = lax.optimization_barrier((oth, last_own))
        last_oth, oth = oth, hop(oth)
        own, last_oth = lax.optimization_barrier((own, last_oth))
        sum_own = sum_own + project(own, distance)
        sum_oth = sum_oth + project(oth, distance)
    far = depth // 2
    early = sum_oth
    last_own = own
    own = hop(own)
    oth, last_own = lax.optimization_barrier((oth, last_own))
    oth, from_up = hop(oth, ring[depth:]), hop(oth, across[:depth])
    early = lax.ppermute(early, "core", [(0, 1)])
    sum_own = sum_own + project(own, far - 1)
    sum_oth = sum_oth + project(oth, far - 1)
    last_own, own = own, hop(own, ring[depth:])
    oth, last_own = lax.optimization_barrier((oth, last_own))
    oth = hop(oth, ring[depth:])
    sum_oth = sum_oth + project(oth, far)
    late = lax.ppermute(sum_oth, "core", [(1, 0)])
    sum_own = sum_own + project(from_up, 1 - far) + project(own, far)
    sum_own, early, late = lax.optimization_barrier((sum_own, early, late))
    return (sum_own + (early + late)).astype(BF16)


def solution(mesh):
    chips = Mesh(mesh.devices.reshape(4, 4, 2, 16), ("y", "x", "core", "ch"))
    seq = ("y", "x", "core")
    placed = (P(seq, "ch"), P(seq, "ch"), P(seq, "ch"), P(None, "ch"), P(None, "ch"), P("ch"), P(None, "ch"))
    return jax.shard_map(body, mesh=chips, in_specs=placed, out_specs=P(seq, "ch"), check_vma=False)
```

```python
import jax
import jax.numpy as jnp
from jax import lax
from jax.experimental import pallas as pl
from jax.experimental.pallas import tpu as pltpu
from jax.sharding import Mesh
from jax.sharding import PartitionSpec as P

BLOCKS = 8
LANES = 128
F32 = jnp.float32
BF16 = jnp.bfloat16


def spread(ref, mode, lanes):
    return jnp.broadcast_to(ref[mode : mode + 1, lanes], (BLOCKS, LANES))


def tree_sum(terms):
    terms = list(terms)
    while len(terms) > 1:
        terms = [a + b for a, b in zip(terms[::2], terms[1::2])]
    return terms[0]


def fetch(pairs, sems):
    copies = [pltpu.make_async_copy(source, target, sems.at[i]) for i, (source, target) in enumerate(pairs)]
    for copy in copies:
        copy.start()
    return copies


def fill(flat, rows, value):
    piece = 64

    @pl.loop(0, rows // piece)
    def _(i):
        at = pl.ds(pl.multiple_of(i * piece, piece), piece)
        now = value(at)
        for half in range(flat.shape[0]):
            flat[half, at, :] = now[:, half * LANES : (half + 1) * LANES]


def mixed_in(k_ref, v_ref):
    return lambda at: (k_ref[at, :].astype(F32) * v_ref[at, :].astype(F32)).astype(BF16).astype(F32)


def block_ends(flat, rates_ref, half):
    modes, steps = rates_ref.shape[0], flat.shape[1] // BLOCKS
    lanes = slice(half * LANES, (half + 1) * LANES)
    poles = [jnp.exp(-spread(rates_ref, m, lanes)) for m in range(modes)]

    def step(j, held):
        now = flat[half, pl.ds(j, BLOCKS, stride=steps), :]
        return tuple(p * h + now for p, h in zip(poles, held))

    return poles, lax.fori_loop(0, steps, step, (jnp.zeros((BLOCKS, LANES), F32),) * modes, unroll=8)


def states_kernel(k_hbm, v_hbm, rates_hbm, every_hbm, total_ref, flat, k_ref, v_ref, rates_ref, sems, sent):
    modes, width = rates_ref.shape
    rows = k_ref.shape[0]
    steps = rows // BLOCKS
    for copy in fetch(((rates_hbm, rates_ref), (k_hbm, k_ref), (v_hbm, v_ref)), sems):
        copy.wait()
    fill(flat, rows, mixed_in(k_ref, v_ref))
    block = lax.broadcasted_iota(jnp.int32, (BLOCKS, LANES), 0).astype(F32)
    for half in range(width // LANES):
        lanes = slice(half * LANES, (half + 1) * LANES)
        _, held = block_ends(flat, rates_ref, half)
        for m in range(modes):
            fade = jnp.exp(-spread(rates_ref, m, lanes) * (steps * (BLOCKS - 1 - block)))
            total_ref[m : m + 1, lanes] = jnp.sum(fade * held[m], axis=0, keepdims=True)
    copies = [pltpu.make_async_copy(total_ref, every_hbm.at[i], sent.at[i]) for i in range(every_hbm.shape[0])]
    for copy in copies:
        copy.start()
    for copy in copies:
        copy.wait()


def local_kernel(k_hbm, v_hbm, q_hbm, rates_hbm, resid_hbm, skip_hbm, out_hbm, flat, flat_q, k_ref, v_ref, q_ref, rates_ref, resid_ref, skip_ref, out_ref, sems):
    modes, width = rates_ref.shape
    rows = q_ref.shape[0]
    steps = rows // BLOCKS
    pairs = ((rates_hbm, rates_ref), (resid_hbm, resid_ref), (skip_hbm, skip_ref))
    for copy in fetch(pairs + ((k_hbm, k_ref), (v_hbm, v_ref), (q_hbm, q_ref)), sems):
        copy.wait()
    fill(flat, rows, mixed_in(k_ref, v_ref))
    fill(flat_q, rows, lambda at: q_ref[at, :].astype(F32))
    block = lax.broadcasted_iota(jnp.int32, (BLOCKS, LANES), 0)
    for half in range(width // LANES):
        lanes = slice(half * LANES, (half + 1) * LANES)
        poles, held = block_ends(flat, rates_ref, half)
        weights, first = [], []
        for m in range(modes):
            rate = spread(rates_ref, m, lanes)
            weights.append(spread(resid_ref, m, lanes))
            scan = jnp.where(block >= 1, pltpu.roll(held[m], 1, 0), 0.0)
            for shift in (1, 2, 4):
                moved = jnp.where(block >= shift, pltpu.roll(scan, shift, 0), 0.0)
                scan = scan + jnp.exp(-rate * float(steps * shift)) * moved
            first.append(scan)
        direct = spread(skip_ref, 0, lanes)

        def step(j, held):
            now = flat[half, pl.ds(j, BLOCKS, stride=steps), :]
            held = tuple(p * h + now for p, h in zip(poles, held))
            out_ref[j, 0:BLOCKS, lanes] = tree_sum(w * h for w, h in zip(weights, held)) + direct * now
            out_ref[j, BLOCKS : 2 * BLOCKS, lanes] = flat_q[half, pl.ds(j, BLOCKS, stride=steps), :]
            return held

        lax.fori_loop(0, steps, step, tuple(first), unroll=4)
    copy = pltpu.make_async_copy(out_ref, out_hbm, sems.at[7])
    copy.start()
    copy.wait()


def gate_kernel(at_ref, all_hbm, rates_hbm, resid_hbm, local_hbm, out_hbm, flat, all_ref, rates_ref, resid_ref, local_ref, out_ref, sems):
    devices, modes, width = all_ref.shape
    steps = local_ref.shape[0]
    rows = out_ref.shape[0]
    small = fetch(((rates_hbm, rates_ref), (resid_hbm, resid_ref), (all_hbm, all_ref), (local_hbm, local_ref)), sems)
    large = small.pop()
    for copy in small:
        copy.wait()
    block = lax.broadcasted_iota(jnp.int32, (BLOCKS, LANES), 0).astype(F32)
    rates = rates_ref[...]
    fade = jnp.exp(-rates * float(rows))
    before = jnp.zeros((modes, width), F32)
    for d in range(devices - 1):
        before = jnp.where(d < at_ref[0], fade * before + all_ref[d], before)
    before = before * resid_ref[...]
    sent = []
    for half in range(width // LANES):
        lanes = slice(half * LANES, (half + 1) * LANES)
        poles, first = [], []
        for m in range(modes):
            rate = spread(rates_ref, m, lanes)
            poles.append(jnp.exp(-rate))
            come = jnp.broadcast_to(before[m : m + 1, lanes], (BLOCKS, LANES))
            first.append(come * jnp.exp(-rate * (steps * block + 1.0)))
        if half == 0:
            large.wait()

        def step(j, held):
            conv = local_ref[j, 0:BLOCKS, lanes] + tree_sum(held)
            flat[half, pl.ds(j, BLOCKS, stride=steps), :] = local_ref[j, BLOCKS : 2 * BLOCKS, lanes] * conv
            return tuple(p * h for p, h in zip(poles, held))

        lax.fori_loop(0, steps, step, tuple(first), unroll=4)
        piece = 64

        @pl.loop(0, rows // piece)
        def _(i):
            at = pl.ds(pl.multiple_of(i * piece, piece), piece)
            out_ref[at, lanes] = flat[half, at, :].astype(BF16)

        sent.append(pltpu.make_async_copy(out_ref.at[:, lanes], out_hbm.at[:, lanes], sems.at[4 + half]))
        sent[-1].start()
    for copy in sent:
        copy.wait()


VMEM = pl.BlockSpec(memory_space=pltpu.VMEM)
ANY = pl.BlockSpec(memory_space=pl.ANY)
SMEM = pl.BlockSpec(memory_space=pltpu.SMEM)


def kernel_call(kernel, name, cost, **kwargs):
    return pl.pallas_call(
        kernel,
        name=name,
        cost_estimate=pl.CostEstimate(flops=cost, bytes_accessed=1 << 20, transcendentals=0),
        **kwargs,
    )


def body(q_branch, k_branch, v_branch, decay_rates, residues, skip_gain, out_weight):
    rows, width = k_branch.shape
    modes = decay_rates.shape[0]
    steps = rows // BLOCKS
    seq = ("y", "x", "core")
    devices = lax.axis_size(seq)
    depth = lax.axis_size("ch")
    core, z = lax.axis_index("core"), lax.axis_index("ch")
    position = lax.axis_index(seq).reshape(1).astype(jnp.int32)
    shape = lambda s, d=F32: jax.ShapeDtypeStruct(s, d)
    flat_shape = (width // LANES, rows, LANES)
    work = modes * rows * width

    flat_of = pltpu.VMEM(flat_shape, F32)
    half_of = pltpu.VMEM((rows, width), BF16)
    modal = pltpu.VMEM((modes, width), F32)
    sems = lambda count: pltpu.SemaphoreType.DMA((count,))

    by_step = (steps, 2 * BLOCKS, width)
    every = kernel_call(
        states_kernel,
        "states",
        2 * work,
        out_shape=shape((devices, modes, width)),
        in_specs=[ANY] * 3,
        out_specs=ANY,
        scratch_shapes=[modal, flat_of, half_of, half_of, modal, sems(3), sems(devices)],
    )(k_branch, v_branch, decay_rates)
    every = lax.all_to_all(every, seq, split_axis=0, concat_axis=0, tiled=True)
    local = kernel_call(
        local_kernel,
        "local_convolution",
        6 * work,
        out_shape=shape(by_step),
        in_specs=[ANY] * 6,
        out_specs=ANY,
        scratch_shapes=[flat_of, flat_of, half_of, half_of, half_of, modal, modal]
        + [pltpu.VMEM((1, width), F32), pltpu.VMEM(by_step, F32), sems(8)],
    )(k_branch, v_branch, q_branch, decay_rates, residues, skip_gain[None, :])
    own = kernel_call(
        gate_kernel,
        "carry_and_gate",
        2 * work,
        out_shape=shape((rows, width), BF16),
        in_specs=[SMEM] + [ANY] * 4,
        out_specs=ANY,
        scratch_shapes=[flat_of, pltpu.VMEM((devices, modes, width), F32), modal, modal]
        + [pltpu.VMEM(by_step, F32), half_of, sems(4 + width // LANES)],
    )(position, every, decay_rates, residues, local)

    ring = [(c * depth + i, c * depth + (i + 1 - 2 * c) % depth) for c in range(2) for i in range(depth)]
    cross = [((1 - c) * depth + i, c * depth + (i + 1 - 2 * c) % depth) for c in range(2) for i in range(depth)]
    across = [(c * depth + i, (1 - c) * depth + (i + 1 - 2 * c) % depth) for c in range(2) for i in range(depth)]
    hop = lambda array, pairs=ring: lax.ppermute(array, ("core", "ch"), pairs)

    def project(array, distance):
        source = lax.rem(z + (2 * core - 1) * distance + depth, depth)
        weight = lax.dynamic_slice(out_weight, (source * width, 0), (width, out_weight.shape[1]))
        return jnp.dot(array, weight, preferred_element_type=F32)

    sum_own = project(own, 0)
    own, oth = hop(own), hop(own, cross)
    sum_own, sum_oth = sum_own + project(own, 1), project(oth, 1)
    last_oth = oth
    for distance in range(2, depth // 2 - 1):
        last_own = own
        own = hop(own)
        oth, last_own = lax.optimization_barrier((oth, last_own))
        last_oth, oth = oth, hop(oth)
        own, last_oth = lax.optimization_barrier((own, last_oth))
        sum_own = sum_own + project(own, distance)
        sum_oth = sum_oth + project(oth, distance)
    far = depth // 2
    early = sum_oth
    last_own = own
    own = hop(own)
    oth, last_own = lax.optimization_barrier((oth, last_own))
    oth, from_up = hop(oth, ring[depth:]), hop(oth, across[:depth])
    early = lax.ppermute(early, "core", [(0, 1)])
    sum_own = sum_own + project(own, far - 1)
    sum_oth = sum_oth + project(oth, far - 1)
    last_own, own = own, hop(own, ring[depth:])
    oth, last_own = lax.optimization_barrier((oth, last_own))
    oth = hop(oth, ring[depth:])
    sum_oth = sum_oth + project(oth, far)
    late = lax.ppermute(sum_oth, "core", [(1, 0)])
    sum_own = sum_own + project(from_up, 1 - far) + project(own, far)
    sum_own, early, late = lax.optimization_barrier((sum_own, early, late))
    return (sum_own + (early + late)).astype(BF16)


def solution(mesh):
    chips = Mesh(mesh.devices.reshape(4, 4, 2, 16), ("y", "x", "core", "ch"))
    seq = ("y", "x", "core")
    placed = (P(seq, "ch"), P(seq, "ch"), P(seq, "ch"), P(None, "ch"), P(None, "ch"), P("ch"), P(None, "ch"))
    return jax.shard_map(body, mesh=chips, in_specs=placed, out_specs=P(seq, "ch"), check_vma=False)
```

```python
import jax
import jax.numpy as jnp
from jax import lax
from jax.experimental import pallas as pl
from jax.experimental.pallas import tpu as pltpu
from jax.sharding import Mesh
from jax.sharding import PartitionSpec as P

BLOCKS = 8
LANES = 128
F32 = jnp.float32
BF16 = jnp.bfloat16


def spread(ref, mode, lanes):
    return jnp.broadcast_to(ref[mode : mode + 1, lanes], (BLOCKS, LANES))


def tree_sum(terms):
    terms = list(terms)
    while len(terms) > 1:
        terms = [a + b for a, b in zip(terms[::2], terms[1::2])]
    return terms[0]


def fetch(pairs, sems):
    copies = [pltpu.make_async_copy(source, target, sems.at[i]) for i, (source, target) in enumerate(pairs)]
    for copy in copies:
        copy.start()
    return copies


def fill(flat, rows, value):
    piece = 64

    @pl.loop(0, rows // piece)
    def _(i):
        at = pl.ds(pl.multiple_of(i * piece, piece), piece)
        now = value(at)
        for half in range(flat.shape[0]):
            flat[half, at, :] = now[:, half * LANES : (half + 1) * LANES]


def mixed_in(k_ref, v_ref):
    return lambda at: (k_ref[at, :].astype(F32) * v_ref[at, :].astype(F32)).astype(BF16).astype(F32)


def block_ends(flat, rates_ref, half):
    modes, steps = rates_ref.shape[0], flat.shape[1] // BLOCKS
    lanes = slice(half * LANES, (half + 1) * LANES)
    poles = [jnp.exp(-spread(rates_ref, m, lanes)) for m in range(modes)]

    def step(j, held):
        now = flat[half, pl.ds(j, BLOCKS, stride=steps), :]
        return tuple(p * h + now for p, h in zip(poles, held))

    return poles, lax.fori_loop(0, steps, step, (jnp.zeros((BLOCKS, LANES), F32),) * modes, unroll=8)


def states_kernel(k_hbm, v_hbm, rates_hbm, every_hbm, total_ref, flat, k_ref, v_ref, rates_ref, sems, sent):
    modes, width = rates_ref.shape
    rows = k_ref.shape[0]
    steps = rows // BLOCKS
    for copy in fetch(((rates_hbm, rates_ref), (k_hbm, k_ref), (v_hbm, v_ref)), sems):
        copy.wait()
    fill(flat, rows, mixed_in(k_ref, v_ref))
    block = lax.broadcasted_iota(jnp.int32, (BLOCKS, LANES), 0).astype(F32)
    for half in range(width // LANES):
        lanes = slice(half * LANES, (half + 1) * LANES)
        _, held = block_ends(flat, rates_ref, half)
        for m in range(modes):
            fade = jnp.exp(-spread(rates_ref, m, lanes) * (steps * (BLOCKS - 1 - block)))
            total_ref[m : m + 1, lanes] = jnp.sum(fade * held[m], axis=0, keepdims=True)
    copies = [pltpu.make_async_copy(total_ref, every_hbm.at[i], sent.at[i]) for i in range(every_hbm.shape[0])]
    for copy in copies:
        copy.start()
    for copy in copies:
        copy.wait()


def local_kernel(k_hbm, v_hbm, q_hbm, rates_hbm, resid_hbm, skip_hbm, out_ref, flat, flat_q, k_ref, v_ref, q_ref, rates_ref, resid_ref, skip_ref, sems):
    modes, width = rates_ref.shape
    rows = q_ref.shape[0]
    steps = rows // BLOCKS
    pairs = ((rates_hbm, rates_ref), (resid_hbm, resid_ref), (skip_hbm, skip_ref))
    for copy in fetch(pairs + ((k_hbm, k_ref), (v_hbm, v_ref), (q_hbm, q_ref)), sems):
        copy.wait()
    fill(flat, rows, mixed_in(k_ref, v_ref))
    fill(flat_q, rows, lambda at: q_ref[at, :].astype(F32))
    block = lax.broadcasted_iota(jnp.int32, (BLOCKS, LANES), 0)
    for half in range(width // LANES):
        lanes = slice(half * LANES, (half + 1) * LANES)
        poles, held = block_ends(flat, rates_ref, half)
        weights, first = [], []
        for m in range(modes):
            rate = spread(rates_ref, m, lanes)
            weights.append(spread(resid_ref, m, lanes))
            scan = jnp.where(block >= 1, pltpu.roll(held[m], 1, 0), 0.0)
            for shift in (1, 2, 4):
                moved = jnp.where(block >= shift, pltpu.roll(scan, shift, 0), 0.0)
                scan = scan + jnp.exp(-rate * float(steps * shift)) * moved
            first.append(scan)
        direct = spread(skip_ref, 0, lanes)

        def step(j, held):
            now = flat[half, pl.ds(j, BLOCKS, stride=steps), :]
            held = tuple(p * h + now for p, h in zip(poles, held))
            out_ref[j, 0:BLOCKS, lanes] = tree_sum(w * h for w, h in zip(weights, held)) + direct * now
            out_ref[j, BLOCKS : 2 * BLOCKS, lanes] = flat_q[half, pl.ds(j, BLOCKS, stride=steps), :]
            return held

        lax.fori_loop(0, steps, step, tuple(first), unroll=4)


def gate_kernel(at_ref, all_ref, rates_ref, resid_ref, local_ref, out_ref, flat):
    devices, modes, width = all_ref.shape
    steps = local_ref.shape[0]
    rows = out_ref.shape[0]
    block = lax.broadcasted_iota(jnp.int32, (BLOCKS, LANES), 0).astype(F32)
    rates = rates_ref[...]
    fade = jnp.exp(-rates * float(rows))
    before = jnp.zeros((modes, width), F32)
    for d in range(devices - 1):
        before = jnp.where(d < at_ref[0], fade * before + all_ref[d], before)
    before = before * resid_ref[...]
    for half in range(width // LANES):
        lanes = slice(half * LANES, (half + 1) * LANES)
        poles, first = [], []
        for m in range(modes):
            rate = spread(rates_ref, m, lanes)
            poles.append(jnp.exp(-rate))
            come = jnp.broadcast_to(before[m : m + 1, lanes], (BLOCKS, LANES))
            first.append(come * jnp.exp(-rate * (steps * block + 1.0)))

        def step(j, held):
            conv = local_ref[j, 0:BLOCKS, lanes] + tree_sum(held)
            flat[half, pl.ds(j, BLOCKS, stride=steps), :] = local_ref[j, BLOCKS : 2 * BLOCKS, lanes] * conv
            return tuple(p * h for p, h in zip(poles, held))

        lax.fori_loop(0, steps, step, tuple(first), unroll=4)
        piece = 64

        @pl.loop(0, rows // piece)
        def _(i):
            at = pl.ds(pl.multiple_of(i * piece, piece), piece)
            out_ref[at, lanes] = flat[half, at, :].astype(BF16)


VMEM = pl.BlockSpec(memory_space=pltpu.VMEM)
ANY = pl.BlockSpec(memory_space=pl.ANY)
SMEM = pl.BlockSpec(memory_space=pltpu.SMEM)


def kernel_call(kernel, name, cost, limit=None, **kwargs):
    return pl.pallas_call(
        kernel,
        name=name,
        compiler_params=pltpu.CompilerParams(vmem_limit_bytes=limit),
        cost_estimate=pl.CostEstimate(flops=cost, bytes_accessed=1 << 20, transcendentals=0),
        **kwargs,
    )


def body(q_branch, k_branch, v_branch, decay_rates, residues, skip_gain, out_weight):
    rows, width = k_branch.shape
    modes = decay_rates.shape[0]
    steps = rows // BLOCKS
    seq = ("y", "x", "core")
    devices = lax.axis_size(seq)
    depth = lax.axis_size("ch")
    core, z = lax.axis_index("core"), lax.axis_index("ch")
    position = lax.axis_index(seq).reshape(1).astype(jnp.int32)
    shape = lambda s, d=F32: jax.ShapeDtypeStruct(s, d)
    flat_shape = (width // LANES, rows, LANES)
    work = modes * rows * width

    flat_of = pltpu.VMEM(flat_shape, F32)
    half_of = pltpu.VMEM((rows, width), BF16)
    modal = pltpu.VMEM((modes, width), F32)
    sems = lambda count: pltpu.SemaphoreType.DMA((count,))

    by_step = (steps, 2 * BLOCKS, width)
    every = kernel_call(
        states_kernel,
        "states",
        2 * work,
        out_shape=shape((devices, modes, width)),
        in_specs=[ANY] * 3,
        out_specs=ANY,
        scratch_shapes=[modal, flat_of, half_of, half_of, modal, sems(3), sems(devices)],
    )(k_branch, v_branch, decay_rates)
    every = lax.all_to_all(every, seq, split_axis=0, concat_axis=0, tiled=True)
    local = kernel_call(
        local_kernel,
        "local_convolution",
        6 * work,
        limit=8 << 20,
        out_shape=shape(by_step),
        in_specs=[ANY] * 6,
        out_specs=VMEM,
        scratch_shapes=[flat_of, flat_of, half_of, half_of, half_of, modal, modal]
        + [pltpu.VMEM((1, width), F32), sems(7)],
    )(k_branch, v_branch, q_branch, decay_rates, residues, skip_gain[None, :])
    own = kernel_call(
        gate_kernel,
        "carry_and_gate",
        2 * work,
        limit=8 << 20,
        out_shape=shape((rows, width), BF16),
        in_specs=[SMEM] + [VMEM] * 4,
        out_specs=VMEM,
        scratch_shapes=[flat_of],
    )(position, every, decay_rates, residues, local)

    ring = [(c * depth + i, c * depth + (i + 1 - 2 * c) % depth) for c in range(2) for i in range(depth)]
    cross = [((1 - c) * depth + i, c * depth + (i + 1 - 2 * c) % depth) for c in range(2) for i in range(depth)]
    across = [(c * depth + i, (1 - c) * depth + (i + 1 - 2 * c) % depth) for c in range(2) for i in range(depth)]
    hop = lambda array, pairs=ring: lax.ppermute(array, ("core", "ch"), pairs)

    def project(array, distance):
        source = lax.rem(z + (2 * core - 1) * distance + depth, depth)
        weight = lax.dynamic_slice(out_weight, (source * width, 0), (width, out_weight.shape[1]))
        return jnp.dot(array, weight, preferred_element_type=F32)

    sum_own = project(own, 0)
    own, oth = hop(own), hop(own, cross)
    sum_own, sum_oth = sum_own + project(own, 1), project(oth, 1)
    last_oth = oth
    for distance in range(2, depth // 2 - 1):
        last_own = own
        own = hop(own)
        oth, last_own = lax.optimization_barrier((oth, last_own))
        last_oth, oth = oth, hop(oth)
        own, last_oth = lax.optimization_barrier((own, last_oth))
        sum_own = sum_own + project(own, distance)
        sum_oth = sum_oth + project(oth, distance)
    far = depth // 2
    early = sum_oth
    last_own = own
    own = hop(own)
    oth, last_own = lax.optimization_barrier((oth, last_own))
    oth, from_up = hop(oth, ring[depth:]), hop(oth, across[:depth])
    early = lax.ppermute(early, "core", [(0, 1)])
    sum_own = sum_own + project(own, far - 1)
    sum_oth = sum_oth + project(oth, far - 1)
    last_own, own = own, hop(own, ring[depth:])
    oth, last_own = lax.optimization_barrier((oth, last_own))
    oth = hop(oth, ring[depth:])
    sum_oth = sum_oth + project(oth, far)
    late = lax.ppermute(sum_oth, "core", [(1, 0)])
    sum_own = sum_own + project(from_up, 1 - far) + project(own, far)
    sum_own, early, late = lax.optimization_barrier((sum_own, early, late))
    return (sum_own + (early + late)).astype(BF16)


def solution(mesh):
    chips = Mesh(mesh.devices.reshape(4, 4, 2, 16), ("y", "x", "core", "ch"))
    seq = ("y", "x", "core")
    placed = (P(seq, "ch"), P(seq, "ch"), P(seq, "ch"), P(None, "ch"), P(None, "ch"), P("ch"), P(None, "ch"))
    return jax.shard_map(body, mesh=chips, in_specs=placed, out_specs=P(seq, "ch"), check_vma=False)
```

```python
import jax
import jax.numpy as jnp
from jax import lax
from jax.experimental import pallas as pl
from jax.experimental.pallas import tpu as pltpu
from jax.sharding import Mesh
from jax.sharding import PartitionSpec as P

BLOCKS = 8
LANES = 128
F32 = jnp.float32
BF16 = jnp.bfloat16


def spread(ref, mode, lanes):
    return jnp.broadcast_to(ref[mode : mode + 1, lanes], (BLOCKS, LANES))


def tree_sum(terms):
    terms = list(terms)
    while len(terms) > 1:
        terms = [a + b for a, b in zip(terms[::2], terms[1::2])]
    return terms[0]


def fetch(pairs, sems):
    copies = [pltpu.make_async_copy(source, target, sems.at[i]) for i, (source, target) in enumerate(pairs)]
    for copy in copies:
        copy.start()
    return copies


def fill(flat, rows, value):
    piece = 64

    @pl.loop(0, rows // piece)
    def _(i):
        at = pl.ds(pl.multiple_of(i * piece, piece), piece)
        now = value(at)
        for half in range(flat.shape[0]):
            flat[half, at, :] = now[:, half * LANES : (half + 1) * LANES]


def mixed_in(k_ref, v_ref):
    return lambda at: (k_ref[at, :].astype(F32) * v_ref[at, :].astype(F32)).astype(BF16).astype(F32)


def block_ends(flat, rates_ref, half):
    modes, steps = rates_ref.shape[0], flat.shape[1] // BLOCKS
    lanes = slice(half * LANES, (half + 1) * LANES)
    poles = [jnp.exp(-spread(rates_ref, m, lanes)) for m in range(modes)]

    def step(j, held):
        now = flat[half, pl.ds(j, BLOCKS, stride=steps), :]
        return tuple(p * h + now for p, h in zip(poles, held))

    return poles, lax.fori_loop(0, steps, step, (jnp.zeros((BLOCKS, LANES), F32),) * modes, unroll=8)


def states_kernel(k_hbm, v_hbm, rates_hbm, every_hbm, total_ref, flat, k_ref, v_ref, rates_ref, sems, sent):
    modes, width = rates_ref.shape
    rows = k_ref.shape[0]
    steps = rows // BLOCKS
    for copy in fetch(((rates_hbm, rates_ref), (k_hbm, k_ref), (v_hbm, v_ref)), sems):
        copy.wait()
    fill(flat, rows, mixed_in(k_ref, v_ref))
    block = lax.broadcasted_iota(jnp.int32, (BLOCKS, LANES), 0).astype(F32)
    for half in range(width // LANES):
        lanes = slice(half * LANES, (half + 1) * LANES)
        _, held = block_ends(flat, rates_ref, half)
        for m in range(modes):
            fade = jnp.exp(-spread(rates_ref, m, lanes) * (steps * (BLOCKS - 1 - block)))
            total_ref[m : m + 1, lanes] = jnp.sum(fade * held[m], axis=0, keepdims=True)
    copies = [pltpu.make_async_copy(total_ref, every_hbm.at[i], sent.at[i]) for i in range(every_hbm.shape[0])]
    for copy in copies:
        copy.start()
    for copy in copies:
        copy.wait()


def local_kernel(k_hbm, v_hbm, q_hbm, rates_hbm, resid_hbm, skip_hbm, out_ref, flat, flat_q, k_ref, v_ref, q_ref, rates_ref, resid_ref, skip_ref, sems):
    modes, width = rates_ref.shape
    rows = q_ref.shape[0]
    steps = rows // BLOCKS
    pairs = ((rates_hbm, rates_ref), (resid_hbm, resid_ref), (skip_hbm, skip_ref))
    for copy in fetch(pairs + ((k_hbm, k_ref), (v_hbm, v_ref), (q_hbm, q_ref)), sems):
        copy.wait()
    fill(flat, rows, mixed_in(k_ref, v_ref))
    fill(flat_q, rows, lambda at: q_ref[at, :].astype(F32))
    block = lax.broadcasted_iota(jnp.int32, (BLOCKS, LANES), 0)
    for half in range(width // LANES):
        lanes = slice(half * LANES, (half + 1) * LANES)
        poles, held = block_ends(flat, rates_ref, half)
        weights, first = [], []
        for m in range(modes):
            rate = spread(rates_ref, m, lanes)
            weights.append(spread(resid_ref, m, lanes))
            scan = jnp.where(block >= 1, pltpu.roll(held[m], 1, 0), 0.0)
            for shift in (1, 2, 4):
                moved = jnp.where(block >= shift, pltpu.roll(scan, shift, 0), 0.0)
                scan = scan + jnp.exp(-rate * float(steps * shift)) * moved
            first.append(scan)
        direct = spread(skip_ref, 0, lanes)

        def step(j, held):
            now = flat[half, pl.ds(j, BLOCKS, stride=steps), :]
            held = tuple(p * h + now for p, h in zip(poles, held))
            out_ref[j, 0:BLOCKS, lanes] = tree_sum(w * h for w, h in zip(weights, held)) + direct * now
            out_ref[j, BLOCKS : 2 * BLOCKS, lanes] = flat_q[half, pl.ds(j, BLOCKS, stride=steps), :]
            return held

        lax.fori_loop(0, steps, step, tuple(first), unroll=4)


def gate_kernel(at_ref, all_hbm, rates_ref, resid_ref, local_ref, out_ref, flat, all_ref, poles_ref, grown_ref, sems):
    devices, modes, width = all_ref.shape
    steps = local_ref.shape[0]
    rows = out_ref.shape[0]
    (copy,) = fetch(((all_hbm, all_ref),), sems)
    block = lax.broadcasted_iota(jnp.int32, (BLOCKS, LANES), 0).astype(F32)
    halves = [slice(half * LANES, (half + 1) * LANES) for half in range(width // LANES)]
    for lanes in halves:
        for m in range(modes):
            rate = spread(rates_ref, m, lanes)
            poles_ref[m, :, lanes] = jnp.exp(-rate)
            grown_ref[m, :, lanes] = spread(resid_ref, m, lanes) * jnp.exp(-rate * (steps * block + 1.0))
    fade = jnp.exp(-rates_ref[...] * float(rows))
    copy.wait()
    before = jnp.zeros((modes, width), F32)
    for d in range(devices - 1):
        before = jnp.where(d < at_ref[0], fade * before + all_ref[d], before)
    for half, lanes in enumerate(halves):
        poles = [poles_ref[m, :, lanes] for m in range(modes)]
        first = [grown_ref[m, :, lanes] * jnp.broadcast_to(before[m : m + 1, lanes], (BLOCKS, LANES)) for m in range(modes)]

        def step(j, held):
            conv = local_ref[j, 0:BLOCKS, lanes] + tree_sum(held)
            flat[half, pl.ds(j, BLOCKS, stride=steps), :] = local_ref[j, BLOCKS : 2 * BLOCKS, lanes] * conv
            return tuple(p * h for p, h in zip(poles, held))

        lax.fori_loop(0, steps, step, tuple(first), unroll=8)
        piece = 128

        @pl.loop(0, rows // piece)
        def _(i):
            at = pl.ds(pl.multiple_of(i * piece, piece), piece)
            out_ref[at, lanes] = flat[half, at, :].astype(BF16)


VMEM = pl.BlockSpec(memory_space=pltpu.VMEM)
ANY = pl.BlockSpec(memory_space=pl.ANY)
SMEM = pl.BlockSpec(memory_space=pltpu.SMEM)


def kernel_call(kernel, name, cost, limit=None, **kwargs):
    return pl.pallas_call(
        kernel,
        name=name,
        compiler_params=pltpu.CompilerParams(vmem_limit_bytes=limit),
        cost_estimate=pl.CostEstimate(flops=cost, bytes_accessed=1 << 20, transcendentals=0),
        **kwargs,
    )


def body(q_branch, k_branch, v_branch, decay_rates, residues, skip_gain, out_weight):
    rows, width = k_branch.shape
    modes = decay_rates.shape[0]
    steps = rows // BLOCKS
    seq = ("y", "x", "core")
    devices = lax.axis_size(seq)
    depth = lax.axis_size("ch")
    core, z = lax.axis_index("core"), lax.axis_index("ch")
    position = lax.axis_index(seq).reshape(1).astype(jnp.int32)
    shape = lambda s, d=F32: jax.ShapeDtypeStruct(s, d)
    flat_shape = (width // LANES, rows, LANES)
    work = modes * rows * width

    flat_of = pltpu.VMEM(flat_shape, F32)
    half_of = pltpu.VMEM((rows, width), BF16)
    modal = pltpu.VMEM((modes, width), F32)
    sems = lambda count: pltpu.SemaphoreType.DMA((count,))

    by_step = (steps, 2 * BLOCKS, width)
    every = kernel_call(
        states_kernel,
        "states",
        2 * work,
        out_shape=shape((devices, modes, width)),
        in_specs=[ANY] * 3,
        out_specs=ANY,
        scratch_shapes=[modal, flat_of, half_of, half_of, modal, sems(3), sems(devices)],
    )(k_branch, v_branch, decay_rates)
    every = lax.all_to_all(every, seq, split_axis=0, concat_axis=0, tiled=True)
    local = kernel_call(
        local_kernel,
        "local_convolution",
        6 * work,
        limit=8 << 20,
        out_shape=shape(by_step),
        in_specs=[ANY] * 6,
        out_specs=VMEM,
        scratch_shapes=[flat_of, flat_of, half_of, half_of, half_of, modal, modal]
        + [pltpu.VMEM((1, width), F32), sems(7)],
    )(k_branch, v_branch, q_branch, decay_rates, residues, skip_gain[None, :])
    own = kernel_call(
        gate_kernel,
        "carry_and_gate",
        2 * work,
        limit=8 << 20,
        out_shape=shape((rows, width), BF16),
        in_specs=[SMEM, ANY] + [VMEM] * 3,
        out_specs=VMEM,
        scratch_shapes=[flat_of, pltpu.VMEM((devices, modes, width), F32)]
        + [pltpu.VMEM((modes, BLOCKS, width), F32)] * 2
        + [sems(1)],
    )(position, every, decay_rates, residues, local)

    ring = [(c * depth + i, c * depth + (i + 1 - 2 * c) % depth) for c in range(2) for i in range(depth)]
    cross = [((1 - c) * depth + i, c * depth + (i + 1 - 2 * c) % depth) for c in range(2) for i in range(depth)]
    across = [(c * depth + i, (1 - c) * depth + (i + 1 - 2 * c) % depth) for c in range(2) for i in range(depth)]
    hop = lambda array, pairs=ring: lax.ppermute(array, ("core", "ch"), pairs)

    def project(array, distance):
        source = lax.rem(z + (2 * core - 1) * distance + depth, depth)
        weight = lax.dynamic_slice(out_weight, (source * width, 0), (width, out_weight.shape[1]))
        return jnp.dot(array, weight, preferred_element_type=F32)

    out_weight, own = lax.optimization_barrier((out_weight, own))
    sum_own = project(own, 0)
    own, oth = hop(own), hop(own, cross)
    sum_own, sum_oth = sum_own + project(own, 1), project(oth, 1)
    last_oth = oth
    for distance in range(2, depth // 2 - 1):
        last_own = own
        own = hop(own)
        oth, last_own = lax.optimization_barrier((oth, last_own))
        last_oth, oth = oth, hop(oth)
        own, last_oth = lax.optimization_barrier((own, last_oth))
        sum_own = sum_own + project(own, distance)
        sum_oth = sum_oth + project(oth, distance)
    far = depth // 2
    early = sum_oth
    last_own = own
    own = hop(own)
    oth, last_own = lax.optimization_barrier((oth, last_own))
    oth, from_up = hop(oth, ring[depth:]), hop(oth, across[:depth])
    early = lax.ppermute(early, "core", [(0, 1)])
    sum_own = sum_own + project(own, far - 1)
    sum_oth = sum_oth + project(oth, far - 1)
    last_own, own = own, hop(own, ring[depth:])
    oth, last_own = lax.optimization_barrier((oth, last_own))
    oth = hop(oth, ring[depth:])
    sum_oth = sum_oth + project(oth, far)
    late = lax.ppermute(sum_oth, "core", [(1, 0)])
    sum_own = sum_own + project(from_up, 1 - far) + project(own, far)
    sum_own, early, late = lax.optimization_barrier((sum_own, early, late))
    return (sum_own + (early + late)).astype(BF16)


def solution(mesh):
    chips = Mesh(mesh.devices.reshape(4, 4, 2, 16), ("y", "x", "core", "ch"))
    seq = ("y", "x", "core")
    placed = (P(seq, "ch"), P(seq, "ch"), P(seq, "ch"), P(None, "ch"), P(None, "ch"), P("ch"), P(None, "ch"))
    return jax.shard_map(body, mesh=chips, in_specs=placed, out_specs=P(seq, "ch"), check_vma=False)
```

```python
import jax
import jax.numpy as jnp
from jax import lax
from jax.experimental import pallas as pl
from jax.experimental.pallas import tpu as pltpu
from jax.sharding import Mesh
from jax.sharding import PartitionSpec as P

BLOCKS = 8
LANES = 128
F32 = jnp.float32
BF16 = jnp.bfloat16


def spread(ref, mode, lanes):
    return jnp.broadcast_to(ref[mode : mode + 1, lanes], (BLOCKS, LANES))


def tree_sum(terms):
    terms = list(terms)
    while len(terms) > 1:
        terms = [a + b for a, b in zip(terms[::2], terms[1::2])]
    return terms[0]


def fetch(pairs, sems):
    copies = [pltpu.make_async_copy(source, target, sems.at[i]) for i, (source, target) in enumerate(pairs)]
    for copy in copies:
        copy.start()
    return copies


def fill(flat, rows, value):
    piece = 64

    @pl.loop(0, rows // piece)
    def _(i):
        at = pl.ds(pl.multiple_of(i * piece, piece), piece)
        now = value(at)
        for half in range(flat.shape[0]):
            flat[half, at, :] = now[:, half * LANES : (half + 1) * LANES]


def mixed_in(k_ref, v_ref):
    return lambda at: (k_ref[at, :].astype(F32) * v_ref[at, :].astype(F32)).astype(BF16).astype(F32)


def block_ends(flat, rates_ref, half):
    modes, steps = rates_ref.shape[0], flat.shape[1] // BLOCKS
    lanes = slice(half * LANES, (half + 1) * LANES)
    poles = [jnp.exp(-spread(rates_ref, m, lanes)) for m in range(modes)]

    def step(j, held):
        now = flat[half, pl.ds(j, BLOCKS, stride=steps), :]
        return tuple(p * h + now for p, h in zip(poles, held))

    return poles, lax.fori_loop(0, steps, step, (jnp.zeros((BLOCKS, LANES), F32),) * modes, unroll=8)


def states_kernel(k_hbm, v_hbm, rates_hbm, every_hbm, total_ref, flat, k_ref, v_ref, rates_ref, poles_ref, fades_ref, sems, sent):
    modes, width = rates_ref.shape
    rows = k_ref.shape[0]
    steps = rows // BLOCKS
    rates_copy, *copies = fetch(((rates_hbm, rates_ref), (k_hbm, k_ref), (v_hbm, v_ref)), sems)
    rates_copy.wait()
    block = lax.broadcasted_iota(jnp.int32, (BLOCKS, LANES), 0).astype(F32)
    halves = [slice(half * LANES, (half + 1) * LANES) for half in range(width // LANES)]
    for lanes in halves:
        for m in range(modes):
            rate = spread(rates_ref, m, lanes)
            poles_ref[m, :, lanes] = jnp.exp(-rate)
            fades_ref[m, :, lanes] = jnp.exp(-rate * (steps * (BLOCKS - 1 - block)))
    for copy in copies:
        copy.wait()
    fill(flat, rows, mixed_in(k_ref, v_ref))
    for half, lanes in enumerate(halves):
        poles = [poles_ref[m, :, lanes] for m in range(modes)]

        def step(j, held):
            now = flat[half, pl.ds(j, BLOCKS, stride=steps), :]
            return tuple(p * h + now for p, h in zip(poles, held))

        held = lax.fori_loop(0, steps, step, (jnp.zeros((BLOCKS, LANES), F32),) * modes, unroll=8)
        for m in range(modes):
            total_ref[m : m + 1, lanes] = jnp.sum(fades_ref[m, :, lanes] * held[m], axis=0, keepdims=True)
    copies = [pltpu.make_async_copy(total_ref, every_hbm.at[i], sent.at[i]) for i in range(every_hbm.shape[0])]
    for copy in copies:
        copy.start()
    for copy in copies:
        copy.wait()


def local_kernel(k_hbm, v_hbm, q_hbm, rates_hbm, resid_hbm, skip_hbm, out_ref, flat, flat_q, k_ref, v_ref, q_ref, rates_ref, resid_ref, skip_ref, sems):
    modes, width = rates_ref.shape
    rows = q_ref.shape[0]
    steps = rows // BLOCKS
    pairs = ((rates_hbm, rates_ref), (resid_hbm, resid_ref), (skip_hbm, skip_ref))
    for copy in fetch(pairs + ((k_hbm, k_ref), (v_hbm, v_ref), (q_hbm, q_ref)), sems):
        copy.wait()
    fill(flat, rows, mixed_in(k_ref, v_ref))
    fill(flat_q, rows, lambda at: q_ref[at, :].astype(F32))
    block = lax.broadcasted_iota(jnp.int32, (BLOCKS, LANES), 0)
    for half in range(width // LANES):
        lanes = slice(half * LANES, (half + 1) * LANES)
        poles, held = block_ends(flat, rates_ref, half)
        weights, first = [], []
        for m in range(modes):
            rate = spread(rates_ref, m, lanes)
            weights.append(spread(resid_ref, m, lanes))
            scan = jnp.where(block >= 1, pltpu.roll(held[m], 1, 0), 0.0)
            for shift in (1, 2, 4):
                moved = jnp.where(block >= shift, pltpu.roll(scan, shift, 0), 0.0)
                scan = scan + jnp.exp(-rate * float(steps * shift)) * moved
            first.append(scan)
        direct = spread(skip_ref, 0, lanes)

        def step(j, held):
            now = flat[half, pl.ds(j, BLOCKS, stride=steps), :]
            held = tuple(p * h + now for p, h in zip(poles, held))
            out_ref[j, 0:BLOCKS, lanes] = tree_sum(w * h for w, h in zip(weights, held)) + direct * now
            out_ref[j, BLOCKS : 2 * BLOCKS, lanes] = flat_q[half, pl.ds(j, BLOCKS, stride=steps), :]
            return held

        lax.fori_loop(0, steps, step, tuple(first), unroll=4)


def gate_kernel(at_ref, all_hbm, rates_ref, resid_ref, local_ref, out_ref, flat, all_ref, poles_ref, grown_ref, sems):
    devices, modes, width = all_ref.shape
    steps = local_ref.shape[0]
    rows = out_ref.shape[0]
    (copy,) = fetch(((all_hbm, all_ref),), sems)
    block = lax.broadcasted_iota(jnp.int32, (BLOCKS, LANES), 0).astype(F32)
    halves = [slice(half * LANES, (half + 1) * LANES) for half in range(width // LANES)]
    for lanes in halves:
        for m in range(modes):
            rate = spread(rates_ref, m, lanes)
            poles_ref[m, :, lanes] = jnp.exp(-rate)
            grown_ref[m, :, lanes] = spread(resid_ref, m, lanes) * jnp.exp(-rate * (steps * block + 1.0))
    fade = jnp.exp(-rates_ref[...] * float(rows))
    copy.wait()
    before = jnp.zeros((modes, width), F32)
    for d in range(devices - 1):
        before = jnp.where(d < at_ref[0], fade * before + all_ref[d], before)
    for half, lanes in enumerate(halves):
        poles = [poles_ref[m, :, lanes] for m in range(modes)]
        first = [grown_ref[m, :, lanes] * jnp.broadcast_to(before[m : m + 1, lanes], (BLOCKS, LANES)) for m in range(modes)]

        def step(j, held):
            conv = local_ref[j, 0:BLOCKS, lanes] + tree_sum(held)
            flat[half, pl.ds(j, BLOCKS, stride=steps), :] = local_ref[j, BLOCKS : 2 * BLOCKS, lanes] * conv
            return tuple(p * h for p, h in zip(poles, held))

        lax.fori_loop(0, steps, step, tuple(first), unroll=8)
        piece = 128

        @pl.loop(0, rows // piece)
        def _(i):
            at = pl.ds(pl.multiple_of(i * piece, piece), piece)
            out_ref[at, lanes] = flat[half, at, :].astype(BF16)


VMEM = pl.BlockSpec(memory_space=pltpu.VMEM)
ANY = pl.BlockSpec(memory_space=pl.ANY)
SMEM = pl.BlockSpec(memory_space=pltpu.SMEM)


def kernel_call(kernel, name, cost, limit=None, **kwargs):
    return pl.pallas_call(
        kernel,
        name=name,
        compiler_params=pltpu.CompilerParams(vmem_limit_bytes=limit),
        cost_estimate=pl.CostEstimate(flops=cost, bytes_accessed=1 << 20, transcendentals=0),
        **kwargs,
    )


def body(q_branch, k_branch, v_branch, decay_rates, residues, skip_gain, out_weight):
    rows, width = k_branch.shape
    modes = decay_rates.shape[0]
    steps = rows // BLOCKS
    seq = ("y", "x", "core")
    devices = lax.axis_size(seq)
    depth = lax.axis_size("ch")
    core, z = lax.axis_index("core"), lax.axis_index("ch")
    position = lax.axis_index(seq).reshape(1).astype(jnp.int32)
    shape = lambda s, d=F32: jax.ShapeDtypeStruct(s, d)
    flat_shape = (width // LANES, rows, LANES)
    work = modes * rows * width

    flat_of = pltpu.VMEM(flat_shape, F32)
    half_of = pltpu.VMEM((rows, width), BF16)
    modal = pltpu.VMEM((modes, width), F32)
    by_block = pltpu.VMEM((modes, BLOCKS, width), F32)
    sems = lambda count: pltpu.SemaphoreType.DMA((count,))

    by_step = (steps, 2 * BLOCKS, width)
    every = kernel_call(
        states_kernel,
        "states",
        2 * work,
        out_shape=shape((devices, modes, width)),
        in_specs=[ANY] * 3,
        out_specs=ANY,
        scratch_shapes=[modal, flat_of, half_of, half_of, modal, by_block, by_block, sems(3), sems(devices)],
    )(k_branch, v_branch, decay_rates)
    every = lax.all_to_all(every, seq, split_axis=0, concat_axis=0, tiled=True)
    local = kernel_call(
        local_kernel,
        "local_convolution",
        6 * work,
        limit=8 << 20,
        out_shape=shape(by_step),
        in_specs=[ANY] * 6,
        out_specs=VMEM,
        scratch_shapes=[flat_of, flat_of, half_of, half_of, half_of, modal, modal]
        + [pltpu.VMEM((1, width), F32), sems(7)],
    )(k_branch, v_branch, q_branch, decay_rates, residues, skip_gain[None, :])
    own = kernel_call(
        gate_kernel,
        "carry_and_gate",
        2 * work,
        limit=8 << 20,
        out_shape=shape((rows, width), BF16),
        in_specs=[SMEM, ANY] + [VMEM] * 3,
        out_specs=VMEM,
        scratch_shapes=[flat_of, pltpu.VMEM((devices, modes, width), F32)]
        + [pltpu.VMEM((modes, BLOCKS, width), F32)] * 2
        + [sems(1)],
    )(position, every, decay_rates, residues, local)

    ring = [(c * depth + i, c * depth + (i + 1 - 2 * c) % depth) for c in range(2) for i in range(depth)]
    cross = [((1 - c) * depth + i, c * depth + (i + 1 - 2 * c) % depth) for c in range(2) for i in range(depth)]
    across = [(c * depth + i, (1 - c) * depth + (i + 1 - 2 * c) % depth) for c in range(2) for i in range(depth)]
    hop = lambda array, pairs=ring: lax.ppermute(array, ("core", "ch"), pairs)

    def project(array, distance):
        source = lax.rem(z + (2 * core - 1) * distance + depth, depth)
        weight = lax.dynamic_slice(out_weight, (source * width, 0), (width, out_weight.shape[1]))
        return jnp.dot(array, weight, preferred_element_type=F32)

    out_weight, own = lax.optimization_barrier((out_weight, own))
    sum_own = project(own, 0)
    own, oth = hop(own), hop(own, cross)
    sum_own, sum_oth = sum_own + project(own, 1), project(oth, 1)
    last_oth = oth
    for distance in range(2, depth // 2 - 1):
        last_own = own
        own = hop(own)
        oth, last_own = lax.optimization_barrier((oth, last_own))
        last_oth, oth = oth, hop(oth)
        own, last_oth = lax.optimization_barrier((own, last_oth))
        sum_own = sum_own + project(own, distance)
        sum_oth = sum_oth + project(oth, distance)
    far = depth // 2
    early = sum_oth
    last_own = own
    own = hop(own)
    oth, last_own = lax.optimization_barrier((oth, last_own))
    oth, from_up = hop(oth, ring[depth:]), hop(oth, across[:depth])
    early = lax.ppermute(early, "core", [(0, 1)])
    sum_own = sum_own + project(own, far - 1)
    sum_oth = sum_oth + project(oth, far - 1)
    last_own, own = own, hop(own, ring[depth:])
    oth, last_own = lax.optimization_barrier((oth, last_own))
    oth = hop(oth, ring[depth:])
    sum_oth = sum_oth + project(oth, far)
    late = lax.ppermute(sum_oth, "core", [(1, 0)])
    sum_own = sum_own + project(from_up, 1 - far) + project(own, far)
    sum_own, early, late = lax.optimization_barrier((sum_own, early, late))
    return (sum_own + (early + late)).astype(BF16)


def solution(mesh):
    chips = Mesh(mesh.devices.reshape(4, 4, 2, 16), ("y", "x", "core", "ch"))
    seq = ("y", "x", "core")
    placed = (P(seq, "ch"), P(seq, "ch"), P(seq, "ch"), P(None, "ch"), P(None, "ch"), P("ch"), P(None, "ch"))
    return jax.shard_map(body, mesh=chips, in_specs=placed, out_specs=P(seq, "ch"), check_vma=False)
```

```python
import jax
import jax.numpy as jnp
from jax import lax
from jax.experimental import pallas as pl
from jax.experimental.pallas import tpu as pltpu
from jax.sharding import Mesh
from jax.sharding import PartitionSpec as P

BLOCKS = 8
LANES = 128
F32 = jnp.float32
BF16 = jnp.bfloat16


def spread(ref, mode, lanes):
    return jnp.broadcast_to(ref[mode : mode + 1, lanes], (BLOCKS, LANES))


def tree_sum(terms):
    terms = list(terms)
    while len(terms) > 1:
        terms = [a + b for a, b in zip(terms[::2], terms[1::2])]
    return terms[0]


def fetch(pairs, sems):
    copies = [pltpu.make_async_copy(source, target, sems.at[i]) for i, (source, target) in enumerate(pairs)]
    for copy in copies:
        copy.start()
    return copies


def fill(flat, rows, value):
    piece = 64

    @pl.loop(0, rows // piece)
    def _(i):
        at = pl.ds(pl.multiple_of(i * piece, piece), piece)
        now = value(at)
        for half in range(flat.shape[0]):
            flat[half, at, :] = now[:, half * LANES : (half + 1) * LANES]


def mixed_in(k_ref, v_ref):
    return lambda at: (k_ref[at, :].astype(F32) * v_ref[at, :].astype(F32)).astype(BF16).astype(F32)


def block_ends(flat, rates_ref, half):
    modes, steps = rates_ref.shape[0], flat.shape[1] // BLOCKS
    lanes = slice(half * LANES, (half + 1) * LANES)
    poles = [jnp.exp(-spread(rates_ref, m, lanes)) for m in range(modes)]

    def step(j, held):
        now = flat[half, pl.ds(j, BLOCKS, stride=steps), :]
        return tuple(p * h + now for p, h in zip(poles, held))

    return poles, lax.fori_loop(0, steps, step, (jnp.zeros((BLOCKS, LANES), F32),) * modes, unroll=8)


def states_kernel(k_hbm, v_hbm, rates_hbm, every_hbm, total_ref, flat, k_ref, v_ref, rates_ref, sems, sent):
    modes, width = rates_ref.shape
    rows = k_ref.shape[0]
    steps = rows // BLOCKS
    for copy in fetch(((rates_hbm, rates_ref), (k_hbm, k_ref), (v_hbm, v_ref)), sems):
        copy.wait()
    fill(flat, rows, mixed_in(k_ref, v_ref))
    block = lax.broadcasted_iota(jnp.int32, (BLOCKS, LANES), 0).astype(F32)
    for half in range(width // LANES):
        lanes = slice(half * LANES, (half + 1) * LANES)
        _, held = block_ends(flat, rates_ref, half)
        for m in range(modes):
            fade = jnp.exp(-spread(rates_ref, m, lanes) * (steps * (BLOCKS - 1 - block)))
            total_ref[m : m + 1, lanes] = jnp.sum(fade * held[m], axis=0, keepdims=True)
    copies = [pltpu.make_async_copy(total_ref, every_hbm.at[i], sent.at[i]) for i in range(every_hbm.shape[0])]
    for copy in copies:
        copy.start()
    for copy in copies:
        copy.wait()


def local_kernel(k_hbm, v_hbm, q_hbm, rates_hbm, resid_hbm, skip_hbm, out_ref, flat, flat_q, k_ref, v_ref, q_ref, rates_ref, resid_ref, skip_ref, sems):
    modes, width = rates_ref.shape
    rows = q_ref.shape[0]
    steps = rows // BLOCKS
    pairs = ((rates_hbm, rates_ref), (resid_hbm, resid_ref), (skip_hbm, skip_ref))
    for copy in fetch(pairs + ((k_hbm, k_ref), (v_hbm, v_ref), (q_hbm, q_ref)), sems):
        copy.wait()
    fill(flat, rows, mixed_in(k_ref, v_ref))
    fill(flat_q, rows, lambda at: q_ref[at, :].astype(F32))
    block = lax.broadcasted_iota(jnp.int32, (BLOCKS, LANES), 0)
    for half in range(width // LANES):
        lanes = slice(half * LANES, (half + 1) * LANES)
        poles, held = block_ends(flat, rates_ref, half)
        weights, first = [], []
        for m in range(modes):
            rate = spread(rates_ref, m, lanes)
            weights.append(spread(resid_ref, m, lanes))
            scan = jnp.where(block >= 1, pltpu.roll(held[m], 1, 0), 0.0)
            for shift in (1, 2, 4):
                moved = jnp.where(block >= shift, pltpu.roll(scan, shift, 0), 0.0)
                scan = scan + jnp.exp(-rate * float(steps * shift)) * moved
            first.append(scan)
        direct = spread(skip_ref, 0, lanes)

        def step(j, held):
            now = flat[half, pl.ds(j, BLOCKS, stride=steps), :]
            held = tuple(p * h + now for p, h in zip(poles, held))
            out_ref[j, 0:BLOCKS, lanes] = tree_sum(w * h for w, h in zip(weights, held)) + direct * now
            out_ref[j, BLOCKS : 2 * BLOCKS, lanes] = flat_q[half, pl.ds(j, BLOCKS, stride=steps), :]
            return held

        lax.fori_loop(0, steps, step, tuple(first), unroll=4)


def gate_kernel(at_ref, all_hbm, rates_ref, resid_ref, local_ref, out_ref, flat, all_ref, poles_ref, grown_ref, sems):
    devices, modes, width = all_ref.shape
    steps = local_ref.shape[0]
    rows = out_ref.shape[0]
    (copy,) = fetch(((all_hbm, all_ref),), sems)
    block = lax.broadcasted_iota(jnp.int32, (BLOCKS, LANES), 0).astype(F32)
    halves = [slice(half * LANES, (half + 1) * LANES) for half in range(width // LANES)]
    for lanes in halves:
        for m in range(modes):
            rate = spread(rates_ref, m, lanes)
            poles_ref[m, :, lanes] = jnp.exp(-rate)
            grown_ref[m, :, lanes] = spread(resid_ref, m, lanes) * jnp.exp(-rate * (steps * block + 1.0))
    fade = jnp.exp(-rates_ref[...] * float(rows))
    copy.wait()
    before = jnp.zeros((modes, width), F32)
    for d in range(devices - 1):
        before = jnp.where(d < at_ref[0], fade * before + all_ref[d], before)
    for half, lanes in enumerate(halves):
        poles = [poles_ref[m, :, lanes] for m in range(modes)]
        first = [grown_ref[m, :, lanes] * jnp.broadcast_to(before[m : m + 1, lanes], (BLOCKS, LANES)) for m in range(modes)]

        def step(j, held):
            conv = local_ref[j, 0:BLOCKS, lanes] + tree_sum(held)
            flat[half, pl.ds(j, BLOCKS, stride=steps), :] = local_ref[j, BLOCKS : 2 * BLOCKS, lanes] * conv
            return tuple(p * h for p, h in zip(poles, held))

        lax.fori_loop(0, steps, step, tuple(first), unroll=8)
        piece = 128

        @pl.loop(0, rows // piece)
        def _(i):
            at = pl.ds(pl.multiple_of(i * piece, piece), piece)
            out_ref[at, lanes] = flat[half, at, :].astype(BF16)


VMEM = pl.BlockSpec(memory_space=pltpu.VMEM)
ANY = pl.BlockSpec(memory_space=pl.ANY)
SMEM = pl.BlockSpec(memory_space=pltpu.SMEM)


def kernel_call(kernel, name, cost, limit=None, **kwargs):
    return pl.pallas_call(
        kernel,
        name=name,
        compiler_params=pltpu.CompilerParams(vmem_limit_bytes=limit),
        cost_estimate=pl.CostEstimate(flops=cost, bytes_accessed=1 << 20, transcendentals=0),
        **kwargs,
    )


def body(q_branch, k_branch, v_branch, decay_rates, residues, skip_gain, out_weight):
    rows, width = k_branch.shape
    modes = decay_rates.shape[0]
    steps = rows // BLOCKS
    seq = ("y", "x", "core")
    devices = lax.axis_size(seq)
    depth = lax.axis_size("ch")
    core, z = lax.axis_index("core"), lax.axis_index("ch")
    position = lax.axis_index(seq).reshape(1).astype(jnp.int32)
    shape = lambda s, d=F32: jax.ShapeDtypeStruct(s, d)
    flat_shape = (width // LANES, rows, LANES)
    work = modes * rows * width

    flat_of = pltpu.VMEM(flat_shape, F32)
    half_of = pltpu.VMEM((rows, width), BF16)
    modal = pltpu.VMEM((modes, width), F32)
    sems = lambda count: pltpu.SemaphoreType.DMA((count,))

    by_step = (steps, 2 * BLOCKS, width)
    every = kernel_call(
        states_kernel,
        "states",
        2 * work,
        out_shape=shape((devices, modes, width)),
        in_specs=[ANY] * 3,
        out_specs=ANY,
        scratch_shapes=[modal, flat_of, half_of, half_of, modal, sems(3), sems(devices)],
    )(k_branch, v_branch, decay_rates)
    every = lax.all_to_all(every, seq, split_axis=0, concat_axis=0, tiled=True)
    local = kernel_call(
        local_kernel,
        "local_convolution",
        6 * work,
        limit=8 << 20,
        out_shape=shape(by_step),
        in_specs=[ANY] * 6,
        out_specs=VMEM,
        scratch_shapes=[flat_of, flat_of, half_of, half_of, half_of, modal, modal]
        + [pltpu.VMEM((1, width), F32), sems(7)],
    )(k_branch, v_branch, q_branch, decay_rates, residues, skip_gain[None, :])
    own = kernel_call(
        gate_kernel,
        "carry_and_gate",
        2 * work,
        limit=8 << 20,
        out_shape=shape((rows, width), BF16),
        in_specs=[SMEM, ANY] + [VMEM] * 3,
        out_specs=VMEM,
        scratch_shapes=[flat_of, pltpu.VMEM((devices, modes, width), F32)]
        + [pltpu.VMEM((modes, BLOCKS, width), F32)] * 2
        + [sems(1)],
    )(position, every, decay_rates, residues, local)

    ring = [(c * depth + i, c * depth + (i + 1 - 2 * c) % depth) for c in range(2) for i in range(depth)]
    cross = [((1 - c) * depth + i, c * depth + (i + 1 - 2 * c) % depth) for c in range(2) for i in range(depth)]
    across = [(c * depth + i, (1 - c) * depth + (i + 1 - 2 * c) % depth) for c in range(2) for i in range(depth)]
    hop = lambda array, pairs=ring: lax.ppermute(array, ("core", "ch"), pairs)

    def project(array, distance):
        source = lax.rem(z + (2 * core - 1) * distance + depth, depth)
        weight = lax.dynamic_slice(out_weight, (source * width, 0), (width, out_weight.shape[1]))
        return jnp.dot(array, weight, preferred_element_type=F32)

    out_weight, own = lax.optimization_barrier((out_weight, own))
    sum_own = project(own, 0)
    own, oth = hop(own), hop(own, cross)
    sum_own, sum_oth = sum_own + project(own, 1), project(oth, 1)
    last_oth = oth
    for distance in range(2, depth // 2 - 1):
        last_own = own
        own = hop(own)
        oth, last_own = lax.optimization_barrier((oth, last_own))
        last_oth, oth = oth, hop(oth)
        own, last_oth = lax.optimization_barrier((own, last_oth))
        sum_own = sum_own + project(own, distance)
        sum_oth = sum_oth + project(oth, distance)
    far = depth // 2
    last_own = own
    own = hop(own)
    oth, last_own = lax.optimization_barrier((oth, last_own))
    oth, from_up = hop(oth, ring[depth:]), hop(oth, across[:depth])
    sum_own = sum_own + project(own, far - 1)
    sum_oth = sum_oth + project(oth, far - 1)
    last_own, own = own, hop(own, ring[depth:])
    oth, last_own = lax.optimization_barrier((oth, last_own))
    oth = hop(oth, ring[depth:])
    sum_oth = sum_oth + project(oth, far)
    swapped = lax.ppermute(sum_oth, "core", [(0, 1), (1, 0)])
    sum_own = sum_own + project(from_up, 1 - far) + project(own, far)
    sum_own, swapped = lax.optimization_barrier((sum_own, swapped))
    return (sum_own + swapped).astype(BF16)


def solution(mesh):
    chips = Mesh(mesh.devices.reshape(4, 4, 2, 16), ("y", "x", "core", "ch"))
    seq = ("y", "x", "core")
    placed = (P(seq, "ch"), P(seq, "ch"), P(seq, "ch"), P(None, "ch"), P(None, "ch"), P("ch"), P(None, "ch"))
    return jax.shard_map(body, mesh=chips, in_specs=placed, out_specs=P(seq, "ch"), check_vma=False)
```
